32 devices in a mesh: lat: 4 (over x, core), items: 8 (over z, y).
Axes of the slice: x: 2, y: 2, z: 4, core: 2. Of those that a mesh axis runs over, the one named last changes fastest.
Arguments:
- tokens: bfloat16 [24, 2, 8, 16, 512], P('items', None, 'lat'), may hold values from -6 to 6
- norm1_gain: bfloat16 [512], replicated, may hold values from 0.5 to 1.5
- norm1_bias: bfloat16 [512], replicated, may hold values from -1 to 1
- qkv_weight: bfloat16 [512, 1536], replicated, may hold values from -0.25 to 0.25
- qv_bias: bfloat16 [2, 512], replicated, may hold values from -1 to 1
- proj_weight: bfloat16 [512, 512], replicated, may hold values from -0.75 to 0.75
- proj_bias: bfloat16 [512], replicated, may hold values from -1 to 1
- norm2_gain: bfloat16 [512], replicated, may hold values from 0.5 to 1.5
- norm2_bias: bfloat16 [512], replicated, may hold values from -1 to 1
- fc1_weight: bfloat16 [512, 2048], replicated, may hold values from -0.25 to 0.25
- fc1_bias: bfloat16 [2048], replicated, may hold values from -1 to 1
- fc2_weight: bfloat16 [2048, 512], replicated, may hold values from -0.125 to 0.125
- fc2_bias: bfloat16 [512], replicated, may hold values from -1 to 1
- cotangent: bfloat16 [24, 2, 8, 16, 512], P('items', None, 'lat'), may hold values from -6 to 6
Outputs:
- mixed: bfloat16 [24, 2, 8, 16, 512], P('items', None, 'lat')
- tokens_grad: bfloat16 [24, 2, 8, 16, 512], P('items', None, 'lat')
- norm1_gain_grad: float32 [512], replicated
- norm1_bias_grad: float32 [512], replicated
- qkv_weight_grad: float32 [512, 1536], replicated
- qv_bias_grad: float32 [2, 512], replicated
- proj_weight_grad: float32 [512, 512], replicated
- proj_bias_grad: float32 [512], replicated
- norm2_gain_grad: float32 [512], replicated
- norm2_bias_grad: float32 [512], replicated
- fc1_weight_grad: float32 [512, 2048], replicated
- fc1_bias_grad: float32 [2048], replicated
- fc2_weight_grad: float32 [2048, 512], replicated
- fc2_bias_grad: float32 [512], replicated
The draws below stay inside these ranges and needn't reach their ends.
All inputs are finite; a program needn't handle non-finite values.
Results may differ from the reference program's by a relative error of at most 0.012.
Values may be sent and summed in bfloat16 or wider, within the bound.
No kernel may reach another device: no remote copies, remote signals or barrier semaphores. Data moves between devices by JAX's collectives and lax.ppermute only.
A program may use at most 128 MiB of HBM per device.

```python
import math
import jax
import jax.numpy as jnp
from jax import lax

D = 512
HEADS = 16
HEAD_DIM = 32
FF = 2048
STEPS = 2
LAT_ROWS = 8
LON = 16
ROW_REACH = 1
COL_REACH = 2
ITEMS = 24


def level_of(rng, shape, shards, low, high):
    def one(dim, shards_of):
        heights = jax.random.uniform(jax.random.fold_in(jax.random.fold_in(rng, 6), dim), (shards_of,), jnp.float32, low / len(shards), high / len(shards))
        return jnp.repeat(jnp.exp(heights), shape[dim] // shards_of).reshape((-1,) + (1,) * (len(shape) - dim - 1))

    loudness = one(*shards[0])
    for cut in shards[1:]:
        loudness = loudness * one(*cut)
    return loudness


def noise(rng, shape, width, most, shards=(), dtype=jnp.bfloat16):
    loudness = level_of(rng, shape, shards, -0.22, 0.18) if shards else 1.0
    array = jax.random.normal(rng, shape, jnp.float32) * width * loudness
    return jnp.minimum(jnp.maximum(array, -most), most).astype(dtype)


def setup_inputs(seed: int = 0) -> dict:
    seeds = jax.random.split(jax.random.key(seed), 15)
    tokens = noise(seeds[0], (ITEMS, STEPS, LAT_ROWS, LON, D), 1.0, 6.0, ((0, 8), (2, 4)))
    norm1_gain = jnp.clip(1.0 + 0.1 * jax.random.normal(seeds[1], (D,), jnp.float32), 0.5, 1.5).astype(jnp.bfloat16)
    norm1_bias = noise(seeds[2], (D,), 0.2, 1.0)
    qkv_weight = noise(seeds[3], (D, 3 * D), D ** -0.5, 0.25)
    qv_bias = noise(seeds[4], (2, D), 0.2, 1.0)
    proj_weight = noise(seeds[5], (D, D), (D // 8) ** -0.5, 0.75)
    proj_bias = noise(seeds[6], (D,), 0.2, 1.0)
    norm2_gain = jnp.clip(1.0 + 0.1 * jax.random.normal(seeds[7], (D,), jnp.float32), 0.5, 1.5).astype(jnp.bfloat16)
    norm2_bias = noise(seeds[8], (D,), 0.2, 1.0)
    fc1_weight = noise(seeds[9], (D, FF), D ** -0.5, 0.25)
    fc1_bias = noise(seeds[10], (FF,), 0.2, 1.0)
    fc2_weight = noise(seeds[11], (FF, D), FF ** -0.5, 0.125)
    fc2_bias = noise(seeds[12], (D,), 0.2, 1.0)
    cotangent = noise(seeds[13], (ITEMS, STEPS, LAT_ROWS, LON, D), 1.0, 6.0, ((0, 8), (2, 4)))
    return {"tokens": tokens, "norm1_gain": norm1_gain, "norm1_bias": norm1_bias, "qkv_weight": qkv_weight, "qv_bias": qv_bias, "proj_weight": proj_weight, "proj_bias": proj_bias, "norm2_gain": norm2_gain, "norm2_bias": norm2_bias, "fc1_weight": fc1_weight, "fc1_bias": fc1_bias, "fc2_weight": fc2_weight, "fc2_bias": fc2_bias, "cotangent": cotangent}


precise = lax.Precision.HIGHEST
epsilon = 1e-06

@jax.custom_vjp
def low(v):
    return lax.optimization_barrier(v.astype(jnp.bfloat16)).astype(jnp.float32)

@jax.custom_vjp
def low_back(v):
    return v

def low_keep(v):
    return (low(v), None)

def low_pass(kept, grad):
    return (grad,)

def back_keep(v):
    return (v, None)

def back_low(kept, grad):
    return (low(grad),)
low.defvjp(low_keep, low_pass)
low_back.defvjp(back_keep, back_low)

def layer_norm(values, gain_vec, shift_vec):
    average = lax.optimization_barrier(jnp.mean(values, axis=-1, keepdims=True))
    centred = values - average
    spread = lax.optimization_barrier(jnp.mean(centred * centred, axis=-1, keepdims=True))
    return centred * lax.rsqrt(spread + epsilon) * gain_vec + shift_vec

def window_mask():
    positions = jnp.arange(STEPS * LAT_ROWS * LON)
    row_of = positions // LON % LAT_ROWS
    col_of = positions % LON
    row_gap = jnp.abs(row_of[:, None] - row_of[None, :])
    col_gap = jnp.abs(col_of[:, None] - col_of[None, :])
    col_gap = jnp.minimum(col_gap, LON - col_gap)
    return (row_gap <= ROW_REACH) & (col_gap <= COL_REACH)

def attend(queries, key_rows, value_rows, window):
    item_count = queries.shape[0]
    seq_len = queries.shape[1]
    query_heads = queries.reshape(item_count, seq_len, HEADS, HEAD_DIM)
    key_heads = key_rows.reshape(item_count, seq_len, HEADS, HEAD_DIM)
    value_heads = value_rows.reshape(item_count, seq_len, HEADS, HEAD_DIM)
    scores = jnp.einsum('bqhd,bkhd->bhqk', query_heads, key_heads, precision=precise) * HEAD_DIM ** (-0.5)
    scores = low_back(scores)
    scores = jnp.where(window, scores, -1e+30)
    soft_weights = low(jax.nn.softmax(scores, axis=-1))
    result = jnp.einsum('bhqk,bkhd->bqhd', soft_weights, value_heads, precision=precise)
    return result.reshape(item_count, seq_len, D)

def forward(block_tokens, params, window):
    norm1_gain, norm1_bias, qkv_weight, qv_bias, proj_weight, proj_bias, norm2_gain, norm2_bias, fc1_weight, fc1_bias, fc2_weight, fc2_bias = params
    normed = low(layer_norm(block_tokens, norm1_gain, norm1_bias))
    joined_qkv = jnp.dot(normed, qkv_weight, precision=precise)
    queries = low_back(low(joined_qkv[..., :D] + qv_bias[0]))
    key_rows = low_back(low(joined_qkv[..., D:2 * D]))
    value_rows = low_back(low(joined_qkv[..., 2 * D:] + qv_bias[1]))
    attended = low_back(low(attend(queries, key_rows, value_rows, window)))
    branch = low_back(jnp.dot(attended, proj_weight, precision=precise) + proj_bias)
    middle = block_tokens + branch
    normed_two = low(layer_norm(middle, norm2_gain, norm2_bias))
    hidden_pre = low_back(jnp.dot(normed_two, fc1_weight, precision=precise) + fc1_bias)
    hidden = low(jax.nn.gelu(hidden_pre, approximate=False))
    branch_two = low_back(jnp.dot(hidden, fc2_weight, precision=precise) + fc2_bias)
    return middle + branch_two

def reference(tokens, norm1_gain, norm1_bias, qkv_weight, qv_bias, proj_weight, proj_bias, norm2_gain, norm2_bias, fc1_weight, fc1_bias, fc2_weight, fc2_bias, cotangent):
    params = tuple((p.astype(jnp.float32) for p in (norm1_gain, norm1_bias, qkv_weight, qv_bias, proj_weight, proj_bias, norm2_gain, norm2_bias, fc1_weight, fc1_bias, fc2_weight, fc2_bias)))
    window = window_mask()
    block_items = math.gcd(ITEMS, 16)
    seq_len = STEPS * LAT_ROWS * LON
    flat_tokens = tokens.astype(jnp.float32).reshape(ITEMS // block_items, block_items, seq_len, D)
    flat_cot = cotangent.astype(jnp.float32).reshape(ITEMS // block_items, block_items, seq_len, D)

    def scan_step(totals, block_pair):
        block_tokens, block_cot = block_pair

        def forward_only(inputs, weights):
            return forward(inputs, weights, window)
        result, pullback = jax.vjp(forward_only, block_tokens, params)
        grad_in, grad_params = pullback(block_cot)
        totals = jax.tree.map(lambda a, b: a + b, totals, grad_params)
        return (totals, (result.astype(jnp.bfloat16), grad_in.astype(jnp.bfloat16)))
    zero_grads = jax.tree.map(jnp.zeros_like, params)
    totals, (outputs, grads_in) = lax.scan(scan_step, zero_grads, (flat_tokens, flat_cot))
    return (outputs.reshape(tokens.shape), grads_in.reshape(tokens.shape), totals[0], totals[1], totals[2], totals[3], totals[4], totals[5], totals[6], totals[7], totals[8], totals[9], totals[10], totals[11])
```

```python
import functools
import math

import jax
import jax.numpy as jnp
from jax import lax
from jax.experimental import pallas as pl
from jax.experimental.pallas import tpu as pltpu
from jax.sharding import PartitionSpec as P

HEAD_DIM = 32
ROW_REACH = 1
COL_REACH = 2
GROUP = 128 // HEAD_DIM
EPSILON = 1e-06
SCALE = HEAD_DIM ** (-0.5)
SQRT_HALF = 0.5**0.5
PHI_SCALE = (2.0 * math.pi) ** (-0.5)
NEGATIVE = -1e30

f32 = jnp.float32
bf16 = jnp.bfloat16
MIB = 1024 * 1024


def dot_nn(left, right):
    return lax.dot_general(left, right, (((1,), (0,)), ((), ())), preferred_element_type=f32)


def dot_nt(left, right):
    return lax.dot_general(left, right, (((1,), (1,)), ((), ())), preferred_element_type=f32)


def dot_tn(left, right):
    return lax.dot_general(left, right, (((0,), (0,)), ((), ())), preferred_element_type=f32)


def normed(values):
    mean = jnp.mean(values, axis=-1, keepdims=True)
    centred = values - mean
    spread = jnp.mean(centred * centred, axis=-1, keepdims=True)
    scale = lax.rsqrt(spread + EPSILON)
    return centred * scale, scale


def norm_back(grad, gain, unit, scale):
    scaled = grad * gain
    first = jnp.mean(scaled, axis=-1, keepdims=True)
    second = jnp.mean(scaled * unit, axis=-1, keepdims=True)
    return scale * (scaled - first - unit * second)


def stack_heads(block, lane_head):
    zero = jnp.zeros_like(block)
    return jnp.concatenate(
        [jnp.where(lane_head == head, block, zero) for head in range(GROUP)], axis=0
    )


def fold_heads(stacked, lane_head, rows):
    total = jnp.where(lane_head == 0, stacked[:rows], 0.0)
    for head in range(1, GROUP):
        total = jnp.where(lane_head == head, stacked[head * rows : (head + 1) * rows], total)
    return total


def block_kernel(
    items,
    tok,
    low,
    high,
    cot,
    vecs,
    wqkv,
    wproj,
    w1,
    w2,
    mask,
    mixed_out,
    a_out,
    o_out,
    c_out,
    g_out,
    du_out,
    dy_out,
    dx1_out,
    dq_out,
    dk_out,
    dv_out,
    to_low,
    to_high,
    small_out,
    kv_ref,
    q_ref,
    p_ref,
    do_ref,
):
    rows, width = tok.shape
    hidden = w1.shape[1]
    side = low.shape[0]
    band = rows // items
    edge = side // items
    groups = width // 128
    lane_head = lax.broadcasted_iota(jnp.int32, (1, 128), 1) // HEAD_DIM

    def vec(index):
        return vecs[index : index + 1, :]

    x = tok[...].astype(f32)
    unit, _ = normed(x)
    a_own = (unit * vec(0) + vec(1)).astype(bf16)
    a_out[...] = a_own
    wide = jnp.concatenate([low[...], high[...]], axis=0).astype(f32)
    unit_wide, _ = normed(wide)
    a_wide = (unit_wide * vec(0) + vec(1)).astype(bf16)
    a_all = jnp.concatenate([a_own, a_wide], axis=0)
    q_ref[...] = (dot_nn(a_own, wqkv[:, :width]) + vec(2)).astype(bf16)
    kv_ref[0] = dot_nn(a_all, wqkv[:, width : 2 * width]).astype(bf16)
    kv_ref[1] = (dot_nn(a_all, wqkv[:, 2 * width :]) + vec(3)).astype(bf16)

    window = jnp.concatenate([mask[...]] * GROUP, axis=0)

    def keys_of(which, item, lanes):
        return jnp.concatenate(
            [
                kv_ref[which, item * band : (item + 1) * band, lanes],
                kv_ref[which, rows + item * edge : rows + (item + 1) * edge, lanes],
                kv_ref[which, rows + side + item * edge : rows + side + (item + 1) * edge, lanes],
            ],
            axis=0,
        )

    for item in range(items):
        for group in range(groups):
            lanes = slice(group * 128, (group + 1) * 128)
            own = slice(item * band, (item + 1) * band)
            queries = stack_heads(q_ref[own, lanes], lane_head)
            scores = dot_nt(queries, keys_of(0, item, lanes)) * SCALE + window
            top = jnp.max(scores, axis=-1, keepdims=True)
            weights = jnp.exp(scores - top)
            total = jnp.sum(weights, axis=-1, keepdims=True)
            soft = weights * (1.0 / total)
            p_ref[item * groups + group] = soft
            mixed_heads = dot_nn(soft.astype(bf16), keys_of(1, item, lanes))
            o_out[own, lanes] = fold_heads(mixed_heads, lane_head, band).astype(bf16)

    x1 = x + dot_nn(o_out[...], wproj[...]) + vec(4)
    unit2, scale2 = normed(x1)
    c_low = (unit2 * vec(5) + vec(6)).astype(bf16)
    c_out[...] = c_low
    cot_low = cot[...]
    branch = jnp.zeros((rows, width), f32)
    dc = jnp.zeros((rows, width), f32)
    for part in range(hidden // width):
        cols = slice(part * width, (part + 1) * width)
        u = dot_nn(c_low, w1[:, cols]) + vec(8 + part)
        cdf = 0.5 + 0.5 * lax.erf(u * SQRT_HALF)
        slope = cdf + u * (jnp.exp(u * u * -0.5) * PHI_SCALE)
        act = (u * cdf).astype(bf16)
        g_out[:, cols] = act
        branch = branch + dot_nn(act, w2[cols, :])
        dh = dot_nt(cot_low, w2[cols, :])
        du_low = (dh * slope).astype(bf16)
        du_out[:, cols] = du_low
        small_out[4 + part : 5 + part, :] = jnp.sum(du_low.astype(f32), axis=0, keepdims=True)
        dc = dc + dot_nt(du_low, w1[:, cols])
    mixed_out[...] = (x1 + branch + vec(7)).astype(bf16)
    cot_wide = cot_low.astype(f32)
    small_out[0:1, :] = jnp.sum(dc * unit2, axis=0, keepdims=True)
    small_out[1:2, :] = jnp.sum(dc, axis=0, keepdims=True)
    small_out[2:3, :] = jnp.sum(cot_wide, axis=0, keepdims=True)
    dx1 = cot_wide + norm_back(dc, vec(5), unit2, scale2)
    dx1_out[...] = dx1
    dy = dx1.astype(bf16)
    dy_out[...] = dy
    small_out[3:4, :] = jnp.sum(dy.astype(f32), axis=0, keepdims=True)
    do_ref[...] = dot_nt(dy, wproj[...]).astype(bf16)

    for item in range(items):
        for group in range(groups):
            lanes = slice(group * 128, (group + 1) * 128)
            own = slice(item * band, (item + 1) * band)
            ends = slice(item * edge, (item + 1) * edge)
            grads = stack_heads(do_ref[own, lanes], lane_head)
            queries = stack_heads(q_ref[own, lanes], lane_head)
            soft = p_ref[item * groups + group]
            dp = dot_nt(grads, keys_of(1, item, lanes))
            inner = jnp.sum(soft * dp, axis=-1, keepdims=True)
            ds = (soft * (dp - inner)).astype(bf16)
            dq = fold_heads(dot_nn(ds, keys_of(0, item, lanes)), lane_head, band) * SCALE
            dq_out[own, lanes] = dq.astype(bf16)
            dk = dot_tn(ds, queries) * SCALE
            dv = dot_tn(soft.astype(bf16), grads)
            dk_out[own, lanes] = dk[:band]
            dv_out[own, lanes] = dv[:band]
            to_low[0, ends, lanes] = dk[band : band + edge].astype(bf16)
            to_low[1, ends, lanes] = dv[band : band + edge].astype(bf16)
            to_high[0, ends, lanes] = dk[band + edge :].astype(bf16)
            to_high[1, ends, lanes] = dv[band + edge :].astype(bf16)


def grad_halves(place, slot_index, shards, left, right, keep, send, lanes=slice(None)):
    half = left.shape[1] // 2
    per = half // shards
    step = min(half, 256)
    core = place[0]
    slot = place[slot_index]
    values = right[...]
    for ref, owner in ((keep, core), (send, 1 - core)):
        for start in range(0, half, step):
            columns = pl.ds(pl.multiple_of(owner * half + start, 128), step)
            product = dot_tn(left[:, columns], values)
            for index in range(step // per):
                spot = pl.multiple_of(((start // per + index) ^ slot) * per, per)
                ref[pl.ds(spot, per), lanes] = product[index * per : (index + 1) * per].astype(bf16)


def mlp_grad_kernel(shards, place, g, cot, c, du, o, dy, keep1, send1, keep2, send2):
    hidden = du.shape[1]
    grad_halves(place, 1, shards, g, cot, keep1, send1)
    grad_halves(place, 2, shards, c, du, keep2, send2, slice(0, hidden))
    grad_halves(place, 2, shards, o, dy, keep2, send2, slice(hidden, hidden + dy.shape[1]))


def qkv_grad_kernel(
    shards,
    lat_dev,
    lon,
    place,
    dq,
    dk,
    dv,
    from_below,
    from_above,
    a_low,
    tok,
    vecs,
    dx1,
    wqkv,
    small_in,
    keep,
    send,
    tokens_out,
    small_out,
    joined,
):
    rows, width = tok.shape
    joined[:, :width] = dq[...]
    for which, grads in ((0, dk), (1, dv)):
        columns = slice((1 + which) * width, (2 + which) * width)
        for strip in range(rows // (lat_dev * lon)):
            edge = slice(strip * lon, (strip + 1) * lon)
            for row in range(lat_dev):
                start = (strip * lat_dev + row) * lon
                value = grads[start : start + lon, :]
                if row == 0:
                    value = value + from_below[which, edge, :].astype(f32)
                if row == lat_dev - 1:
                    value = value + from_above[which, edge, :].astype(f32)
                joined[start : start + lon, columns] = value.astype(bf16)
    grad_halves(place, 3, shards, a_low, joined, keep, send)
    da = dot_nt(joined[...], wqkv[...])
    unit, scale = normed(tok[...].astype(f32))
    grad = dx1[...] + norm_back(da, vecs[0:1, :], unit, scale)
    tokens_out[...] = grad.astype(bf16)
    sums = [
        jnp.sum(da * unit, axis=0, keepdims=True),
        jnp.sum(da, axis=0, keepdims=True),
        jnp.sum(joined[:, :width].astype(f32), axis=0, keepdims=True),
        jnp.sum(joined[:, 2 * width :].astype(f32), axis=0, keepdims=True),
    ] + [small_in[index : index + 1, :] for index in range(small_in.shape[0])]
    for index, row in enumerate(sums):
        place_of = slice(index % 3 * width, (index % 3 + 1) * width)
        small_out[index // 3 : index // 3 + 1, place_of] = row.astype(bf16)


def spread_kernel(slot_index, shards, splits, place, own, other, *outs):
    half = own.shape[0]
    per = half // shards
    core = place[0]
    slot = place[slot_index]
    for ref, owner in ((own, core), (other, 1 - core)):
        for index in range(shards):
            spot = pl.multiple_of(owner * half + (index ^ slot) * per, per)
            first = 0
            for out, count in zip(outs, splits):
                out[pl.ds(spot, per), :] = ref[
                    index * per : (index + 1) * per, first : first + count
                ].astype(f32)
                first += count


def on_device(kernel, outs, scratch=(), scalars=0, args=0, vmem=24):
    return pl.pallas_call(
        kernel,
        out_shape=[jax.ShapeDtypeStruct(shape, dtype) for shape, dtype in outs],
        in_specs=[pl.BlockSpec(memory_space=pltpu.SMEM)] * scalars
        + [pl.BlockSpec(memory_space=pltpu.VMEM)] * args,
        out_specs=[pl.BlockSpec(memory_space=pltpu.VMEM)] * len(outs),
        scratch_shapes=list(scratch),
        compiler_params=pltpu.CompilerParams(vmem_limit_bytes=vmem * MIB),
    )


class Axes:
    def __init__(self, mesh):
        self.sizes = dict(mesh.shape)
        bits = self.sizes["items"].bit_length() - 1
        self.core = ("lat", 1)
        chips = ("lat", 2)
        first = ("items", 1)
        second = ("items", 2)
        self.doubled = [("items", 1 << bit) for bit in range(2, bits)]
        self.orders = (
            (chips, first, second),
            (first, second, chips),
            (second, chips, first),
        )

    def bit(self, dim):
        axis, value = dim
        return (lax.axis_index(axis) // value) % 2

    def slot(self, order):
        total = 0
        for dim in order:
            total = total * 2 + self.bit(dim)
        return total

    def exchange(self, value, dim):
        axis, bit = dim
        pairs = [(index, index ^ bit) for index in range(self.sizes[axis])]
        return lax.ppermute(value, axis, pairs)


def add_rows(terms, low, high):
    total = terms[0][low:high].astype(f32)
    for term in terms[1:]:
        total = total + term[low:high].astype(f32)
    return total


def reduce_stream(axes, keep, send, order, small=None):
    terms = [keep, axes.exchange(send, axes.core)]
    if small is not None:
        small = small.astype(f32) + axes.exchange(small, axes.core).astype(f32)
    rows = keep.shape[0]
    extra = 0 if small is None else small.shape[0]

    def swap(value, dim, small):
        if small is None:
            return axes.exchange(value, dim), None
        small_low = small.astype(bf16)
        count = value.shape[0]
        got = axes.exchange(jnp.concatenate([value, small_low], axis=0), dim)
        return got[:count], small_low.astype(f32) + got[count : count + extra].astype(f32)

    for dim in order:
        rows //= 2
        got, small = swap(add_rows(terms, rows, 2 * rows).astype(bf16), dim, small)
        terms.append(got)
    piece = add_rows(terms, 0, rows).astype(bf16)
    for dim in axes.doubled:
        got, small = swap(piece, dim, small)
        piece = (piece.astype(f32) + got.astype(f32)).astype(bf16)
    return piece, small


def gather_stream(axes, piece, order):
    for dim in reversed(order):
        piece = jnp.concatenate([piece, axes.exchange(piece, dim)], axis=0)
    return piece, axes.exchange(piece, axes.core)


def window_mask(lat_index, lat_total, lat_dev, steps, lon):
    query = jnp.arange(steps * lat_dev * lon)
    query_row = query // lon % lat_dev
    query_col = query % lon
    side = jnp.arange(steps * lon)
    key_row = jnp.concatenate(
        [query_row, jnp.full_like(side, -1), jnp.full_like(side, lat_dev)]
    )
    key_col = jnp.concatenate([query_col, side % lon, side % lon])
    gap = jnp.abs(query_col[:, None] - key_col[None, :])
    gap = jnp.minimum(gap, lon - gap)
    near = jnp.abs(query_row[:, None] - key_row[None, :]) <= ROW_REACH
    world_row = lat_index * lat_dev + key_row
    inside = (world_row >= 0) & (world_row < lat_total * lat_dev)
    return jnp.where(near & (gap <= COL_REACH) & inside[None, :], 0.0, NEGATIVE).astype(f32)


def body(
    axes,
    tokens,
    norm1_gain,
    norm1_bias,
    qkv_weight,
    qv_bias,
    proj_weight,
    proj_bias,
    norm2_gain,
    norm2_bias,
    fc1_weight,
    fc1_bias,
    fc2_weight,
    fc2_bias,
    cotangent,
):
    items, steps, lat_dev, lon, width = tokens.shape
    hidden = fc1_weight.shape[1]
    rows = items * steps * lat_dev * lon
    side = items * steps * lon
    lat_total = axes.sizes["lat"]
    shards = 8
    upward = [(index, index + 1) for index in range(lat_total - 1)]
    downward = [(index + 1, index) for index in range(lat_total - 1)]
    low = lax.ppermute(tokens[:, :, lat_dev - 1].reshape(side, width), "lat", upward)
    high = lax.ppermute(tokens[:, :, 0].reshape(side, width), "lat", downward)
    vecs = (
        jnp.concatenate(
            [
                norm1_gain,
                norm1_bias,
                qv_bias.reshape(2 * width),
                proj_bias,
                norm2_gain,
                norm2_bias,
                fc2_bias,
                fc1_bias,
            ]
        )
        .astype(f32)
        .reshape(8 + hidden // width, width)
    )
    mask = window_mask(lax.axis_index("lat"), lat_total, lat_dev, steps, lon)
    place = jnp.stack([axes.bit(axes.core)] + [axes.slot(order) for order in axes.orders])
    flat_tokens = tokens.reshape(rows, width)
    flat_cot = cotangent.reshape(rows, width)
    band = rows // items
    keys = band + 2 * side // items
    groups = width // 128

    (mixed, a_low, o_low, c_low, g_low, du_low, dy_low, dx1, dq, dk, dv, to_low, to_high, small) = on_device(
        functools.partial(block_kernel, items),
        [
            ((rows, width), bf16),
            ((rows, width), bf16),
            ((rows, width), bf16),
            ((rows, width), bf16),
            ((rows, hidden), bf16),
            ((rows, hidden), bf16),
            ((rows, width), bf16),
            ((rows, width), f32),
            ((rows, width), bf16),
            ((rows, width), f32),
            ((rows, width), f32),
            ((2, side, width), bf16),
            ((2, side, width), bf16),
            ((4 + hidden // width, width), f32),
        ],
        scratch=[
            pltpu.VMEM((2, rows + 2 * side, width), bf16),
            pltpu.VMEM((rows, width), bf16),
            pltpu.VMEM((items * groups, GROUP * band, keys), f32),
            pltpu.VMEM((rows, width), bf16),
        ],
        args=10,
        vmem=40,
    )(flat_tokens, low, high, flat_cot, vecs, qkv_weight, proj_weight, fc1_weight, fc2_weight, mask)

    from_above = lax.ppermute(to_low, "lat", downward)
    from_below = lax.ppermute(to_high, "lat", upward)

    both = hidden + width
    keep1, send1, keep2, send2 = on_device(
        functools.partial(mlp_grad_kernel, shards),
        [((hidden // 2, width), bf16)] * 2 + [((width // 2, both), bf16)] * 2,
        scalars=1,
        args=6,
    )(place, g_low, flat_cot, c_low, du_low, o_low, dy_low)

    keep3, send3, tokens_grad, small = on_device(
        functools.partial(qkv_grad_kernel, shards, lat_dev, lon),
        [
            ((width // 2, 3 * width), bf16),
            ((width // 2, 3 * width), bf16),
            ((rows, width), bf16),
            (((8 + hidden // width) // 3, 3 * width), bf16),
        ],
        scratch=[pltpu.VMEM((rows, 3 * width), bf16)],
        scalars=1,
        args=11,
    )(place, dq, dk, dv, from_below, from_above, a_low, flat_tokens, vecs, dx1, qkv_weight, small)

    piece1, _ = reduce_stream(axes, keep1, send1, axes.orders[0])
    piece2, _ = reduce_stream(axes, keep2, send2, axes.orders[1])
    piece3, small = reduce_stream(axes, keep3, send3, axes.orders[2], small)
    halves1 = gather_stream(axes, piece1, axes.orders[0])
    halves2 = gather_stream(axes, piece2, axes.orders[1])
    halves3 = gather_stream(axes, piece3, axes.orders[2])

    def spread(index, halves, splits):
        return on_device(
            functools.partial(spread_kernel, index, shards, splits),
            [((2 * halves[0].shape[0], count), f32) for count in splits],
            scalars=1,
            args=2,
        )(place, *halves)

    (grad_fc2,) = spread(1, halves1, (width,))
    grad_fc1, grad_proj = spread(2, halves2, (hidden, width))
    (grad_qkv,) = spread(3, halves3, (3 * width,))
    small = small.reshape(8 + hidden // width, width)
    return (
        mixed.reshape(tokens.shape),
        tokens_grad.reshape(tokens.shape),
        small[0],
        small[1],
        grad_qkv,
        small[2:4],
        grad_proj,
        small[7],
        small[4],
        small[5],
        grad_fc1,
        small[8:].reshape(hidden),
        grad_fc2,
        small[6],
    )


def solution(mesh):
    split = P("items", None, "lat", None, None)
    whole = P()
    return jax.shard_map(
        functools.partial(body, Axes(mesh)),
        mesh=mesh,
        in_specs=(split,) + (whole,) * 12 + (split,),
        out_specs=(split, split) + (whole,) * 12,
        check_vma=False,
    )
```

```python
import functools
import math

import jax
import jax.numpy as jnp
from jax import lax
from jax.experimental import pallas as pl
from jax.experimental.pallas import tpu as pltpu
from jax.sharding import PartitionSpec as P

HEAD_DIM = 32
ROW_REACH = 1
COL_REACH = 2
GROUP = 128 // HEAD_DIM
EPSILON = 1e-06
SCALE = HEAD_DIM ** (-0.5)
SQRT_HALF = 0.5**0.5
PHI_SCALE = (2.0 * math.pi) ** (-0.5)
NEGATIVE = -1e30
ORDERS = (("zxyw", "xyzw"), ("zywx", "yzxw"), ("yxwz", "xywz"))
ORDER = (2, 3, 1, 3, 2, 1, 3, 2, 1, 3, 2, 1, 3, 2, 1, 3, 2, 3, 1, 2, 3, 1, 3, 2, 1, 3, 2, 1, 3)

f32 = jnp.float32
bf16 = jnp.bfloat16
MIB = 1024 * 1024


def dot_nn(left, right):
    return lax.dot_general(left, right, (((1,), (0,)), ((), ())), preferred_element_type=f32)


def dot_nt(left, right):
    return lax.dot_general(left, right, (((1,), (1,)), ((), ())), preferred_element_type=f32)


def dot_tn(left, right):
    return lax.dot_general(left, right, (((0,), (0,)), ((), ())), preferred_element_type=f32)


def normed(values):
    mean = jnp.mean(values, axis=-1, keepdims=True)
    centred = values - mean
    spread = jnp.mean(centred * centred, axis=-1, keepdims=True)
    scale = lax.rsqrt(spread + EPSILON)
    return centred * scale, scale


def norm_back(grad, gain, unit, scale):
    scaled = grad * gain
    first = jnp.mean(scaled, axis=-1, keepdims=True)
    second = jnp.mean(scaled * unit, axis=-1, keepdims=True)
    return scale * (scaled - first - unit * second)


def as_row(ref):
    return ref[...].astype(f32).reshape(1, ref.shape[0])


def stack_heads(block, lane_head):
    zero = jnp.zeros_like(block)
    return jnp.concatenate(
        [jnp.where(lane_head == head, block, zero) for head in range(GROUP)], axis=0
    )


def fold_heads(stacked, lane_head, rows):
    total = jnp.where(lane_head == 0, stacked[:rows], 0.0)
    for head in range(1, GROUP):
        total = jnp.where(lane_head == head, stacked[head * rows : (head + 1) * rows], total)
    return total


def window_bias(axes, steps, lat_dev, lon):
    band = steps * lat_dev * lon
    keys = band + 2 * steps * lon
    query = lax.broadcasted_iota(jnp.int32, (band, keys), 0)
    key = lax.broadcasted_iota(jnp.int32, (band, keys), 1)
    query_row = query // lon % lat_dev
    first = jnp.where(axes.has_below(), -1, -2 - ROW_REACH)
    last = jnp.where(axes.has_above(), lat_dev, lat_dev + 1 + ROW_REACH)
    key_row = jnp.where(
        key < band, key // lon % lat_dev, jnp.where(key < band + steps * lon, first, last)
    )
    gap = jnp.abs(query % lon - key % lon)
    gap = jnp.minimum(gap, lon - gap)
    seen = (jnp.abs(query_row - key_row) <= ROW_REACH) & (gap <= COL_REACH)
    return jnp.where(seen, 0.0, NEGATIVE)


def block_kernel(
    axes,
    shards,
    items,
    steps,
    lat_dev,
    lon,
    *refs,
):
    sources, finals, refs = refs[:16], refs[16:29], refs[29:]
    targets, locals_, refs = refs[:16], refs[16:29], refs[29:]
    kv_ref, q_ref, p_ref, do_ref, o_ref, c_ref, g_ref, du_ref, dy_ref, in_sems, out_sems = refs
    fetches = start_copies(sources, targets, in_sems)
    (tok, gain1, bias1, qv_bias, beside, across, wqkv, wproj) = targets[:8]
    (bproj, gain2, bias2, w1, b1, w2, b2, cot) = targets[8:]
    (mixed_out, a_out, dx1_out, small_out, keep1, send1, keep2, send2) = locals_[:8]
    (dq_out, dk_out, dv_out, to_beside, to_across) = locals_[8:]
    leaving = []

    def leave(index, slot=0, window=None):
        source, target = locals_[index], finals[index]
        if window is not None:
            source, target = source.at[window], target.at[window]
        copy = pltpu.make_async_copy(source, target, out_sems.at[index, slot])
        copy.start()
        leaving.append(copy)

    for copy in fetches[:6]:
        copy.wait()
    rows, width = tok.shape
    hidden = w1.shape[1]
    side = beside.shape[0]
    band = rows // items
    edge = side // items
    groups = width // 128
    lane_head = lax.broadcasted_iota(jnp.int32, (1, 128), 1) // HEAD_DIM

    g1 = as_row(gain1)
    h1 = as_row(bias1)
    x = tok[...].astype(f32)
    unit, _ = normed(x)
    a_own = (unit * g1 + h1).astype(bf16)
    a_out[...] = a_own
    leave(1)
    wide = jnp.concatenate([beside[...], across[...]], axis=0).astype(f32)
    unit_wide, _ = normed(wide)
    a_wide = (unit_wide * g1 + h1).astype(bf16)
    a_all = jnp.concatenate([a_own, a_wide], axis=0)
    fetches[6].wait()
    q_ref[...] = (dot_nn(a_own, wqkv[:, :width]) + qv_bias[0:1, :].astype(f32)).astype(bf16)
    kv_ref[0] = dot_nn(a_all, wqkv[:, width : 2 * width]).astype(bf16)
    kv_ref[1] = (dot_nn(a_all, wqkv[:, 2 * width :]) + qv_bias[1:2, :].astype(f32)).astype(bf16)

    window = jnp.concatenate([window_bias(axes, steps, lat_dev, lon)] * GROUP, axis=0)
    odd = axes.bit(axes.core)
    below = pl.multiple_of(rows + (1 - odd) * side, 16)
    above = pl.multiple_of(rows + odd * side, 16)

    def keys_of(which, item, lanes):
        return jnp.concatenate(
            [
                kv_ref[which, item * band : (item + 1) * band, lanes],
                kv_ref[which, pl.ds(below + item * edge, edge), lanes],
                kv_ref[which, pl.ds(above + item * edge, edge), lanes],
            ],
            axis=0,
        )

    for item in range(items):
        for group in range(groups):
            lanes = slice(group * 128, (group + 1) * 128)
            own = slice(item * band, (item + 1) * band)
            queries = stack_heads(q_ref[own, lanes], lane_head)
            scores = dot_nt(queries, keys_of(0, item, lanes)) * SCALE + window
            top = jnp.max(scores, axis=-1, keepdims=True)
            weights = jnp.exp(scores - top)
            total = jnp.sum(weights, axis=-1, keepdims=True)
            soft = weights * (1.0 / total)
            p_ref[item * groups + group] = soft
            mixed_heads = dot_nn(soft.astype(bf16), keys_of(1, item, lanes))
            o_ref[own, lanes] = fold_heads(mixed_heads, lane_head, band).astype(bf16)

    for copy in fetches[7:]:
        copy.wait()
    g2 = as_row(gain2)
    h2 = as_row(bias2)
    x1 = x + dot_nn(o_ref[...], wproj[...]) + as_row(bproj)
    unit2, scale2 = normed(x1)
    c_low = (unit2 * g2 + h2).astype(bf16)
    c_ref[...] = c_low
    cot_low = cot[...]
    branch = jnp.zeros((rows, width), f32)
    dc = jnp.zeros((rows, width), f32)
    b1_row = as_row(b1)
    for part in range(hidden // width):
        cols = slice(part * width, (part + 1) * width)
        u = dot_nn(c_low, w1[:, cols]) + b1_row[:, cols]
        cdf = 0.5 + 0.5 * lax.erf(u * SQRT_HALF)
        slope = cdf + u * (jnp.exp(u * u * -0.5) * PHI_SCALE)
        act = (u * cdf).astype(bf16)
        g_ref[:, cols] = act
        branch = branch + dot_nn(act, w2[cols, :])
        dh = dot_nt(cot_low, w2[cols, :])
        du_low = (dh * slope).astype(bf16)
        du_ref[:, cols] = du_low
        small_out[4 + part : 5 + part, :] = jnp.sum(du_low.astype(f32), axis=0, keepdims=True)
        dc = dc + dot_nt(du_low, w1[:, cols])
    mixed_out[...] = (x1 + branch + as_row(b2)).astype(bf16)
    cot_wide = cot_low.astype(f32)
    small_out[0:1, :] = jnp.sum(dc * unit2, axis=0, keepdims=True)
    small_out[1:2, :] = jnp.sum(dc, axis=0, keepdims=True)
    small_out[2:3, :] = jnp.sum(cot_wide, axis=0, keepdims=True)
    dx1 = cot_wide + norm_back(dc, g2, unit2, scale2)
    dx1_out[...] = dx1
    leave(0)
    leave(2)
    dy = dx1.astype(bf16)
    dy_ref[...] = dy
    small_out[3:4, :] = jnp.sum(dy.astype(f32), axis=0, keepdims=True)
    do_ref[...] = dot_nt(dy, wproj[...]).astype(bf16)
    leave(3)
    grad_halves(axes, 0, shards, g_ref, cot, keep1, send1)
    leave(4)
    leave(5)
    grad_halves(axes, 1, shards, c_ref, du_ref, keep2, send2, slice(0, hidden))
    grad_halves(axes, 1, shards, o_ref, dy_ref, keep2, send2, slice(hidden, hidden + width))
    leave(6)
    leave(7)

    for item in range(items):
        for group in range(groups):
            lanes = slice(group * 128, (group + 1) * 128)
            own = slice(item * band, (item + 1) * band)
            ends = slice(item * edge, (item + 1) * edge)
            grads = stack_heads(do_ref[own, lanes], lane_head)
            queries = stack_heads(q_ref[own, lanes], lane_head)
            soft = p_ref[item * groups + group]
            dp = dot_nt(grads, keys_of(1, item, lanes))
            inner = jnp.sum(soft * dp, axis=-1, keepdims=True)
            ds = (soft * (dp - inner)).astype(bf16)
            dq = fold_heads(dot_nn(ds, keys_of(0, item, lanes)), lane_head, band) * SCALE
            dq_out[own, lanes] = dq.astype(bf16)
            dk = dot_tn(ds, queries) * SCALE
            dv = dot_tn(soft.astype(bf16), grads)
            dk_out[own, lanes] = dk[:band]
            dv_out[own, lanes] = dv[:band]
            for index, grad in ((0, dk), (1, dv)):
                down = grad[band : band + edge]
                up = grad[band + edge :]
                to_beside[index, ends, lanes] = jnp.where(odd == 1, down, up).astype(bf16)
                to_across[index, ends, lanes] = jnp.where(odd == 1, up, down).astype(bf16)
        for index in (8, 9, 10):
            leave(index, item, (own, slice(None)))
        for index in (11, 12):
            leave(index, item, (slice(None), ends, slice(None)))
    for copy in leaving:
        copy.wait()


def start_copies(sources, targets, sems, first=0):
    copies = [
        pltpu.make_async_copy(source, target, sems.at[first + index])
        for index, (source, target) in enumerate(zip(sources, targets))
    ]
    for copy in copies:
        copy.start()
    return copies


def grad_halves(axes, stream, shards, left, right, keep, send, lanes=slice(None)):
    half = left.shape[1] // 2
    per = half // shards
    step = min(half, 256)
    core = axes.bit(axes.core)
    values = right[...]
    for ref, owner in ((keep, core), (send, 1 - core)):
        slot = axes.slot(stream, owner)
        for start in range(0, half, step):
            columns = pl.ds(pl.multiple_of(owner * half + start, 128), step)
            product = dot_tn(left[:, columns], values)
            for index in range(step // per):
                spot = pl.multiple_of(((start // per + index) ^ slot) * per, per)
                ref[pl.ds(spot, per), lanes] = product[index * per : (index + 1) * per].astype(bf16)


def qkv_grad_kernel(
    axes,
    shards,
    lat_dev,
    lon,
    *refs,
):
    sources, finals, refs = refs[:11], refs[11:15], refs[15:]
    targets, locals_, refs = refs[:11], refs[11:15], refs[15:]
    joined, in_sems, out_sems = refs
    fetches = start_copies(sources, targets, in_sems)
    dq, dk, dv, from_beside, from_across, a_low, wqkv, tok, gain1, dx1, small_in = targets
    keep, send, tokens_out, small_out = locals_
    for copy in fetches[:6]:
        copy.wait()
    rows, width = tok.shape
    joined[:, :width] = dq[...]
    odd = axes.bit(axes.core) == 1
    for which, grads in ((0, dk), (1, dv)):
        columns = slice((1 + which) * width, (2 + which) * width)
        for strip in range(rows // (lat_dev * lon)):
            edge = slice(strip * lon, (strip + 1) * lon)
            for row in range(lat_dev):
                start = (strip * lat_dev + row) * lon
                value = grads[start : start + lon, :]
                near = from_beside[which, edge, :].astype(f32)
                far = from_across[which, edge, :].astype(f32)
                if row == 0:
                    value = value + jnp.where(odd, near, far)
                if row == lat_dev - 1:
                    value = value + jnp.where(odd, far, near)
                joined[start : start + lon, columns] = value.astype(bf16)
    grad_halves(axes, 2, shards, a_low, joined, keep, send)
    leaving = start_copies(locals_[:2], finals[:2], out_sems)
    for copy in fetches[6:]:
        copy.wait()
    da = dot_nt(joined[...], wqkv[...])
    unit, scale = normed(tok[...].astype(f32))
    grad = dx1[...] + norm_back(da, as_row(gain1), unit, scale)
    tokens_out[...] = grad.astype(bf16)
    sums = [
        jnp.sum(da * unit, axis=0, keepdims=True),
        jnp.sum(da, axis=0, keepdims=True),
        jnp.sum(joined[:, :width].astype(f32), axis=0, keepdims=True),
        jnp.sum(joined[:, 2 * width :].astype(f32), axis=0, keepdims=True),
    ] + [small_in[index : index + 1, :] for index in range(small_in.shape[0])]
    for index, row in enumerate(sums):
        place_of = slice(index % 3 * width, (index % 3 + 1) * width)
        small_out[index // 3 : index // 3 + 1, place_of] = row.astype(bf16)
    leaving += start_copies(locals_[2:], finals[2:], out_sems, 2)
    for copy in leaving:
        copy.wait()


def spread_kernel(axes, stream, shards, splits, other, piece, *refs):
    count = len(splits)
    outs, wide, sems = refs[-2 * count - 1 : -count - 1], refs[-count - 1 : -1], refs[-1]
    half = piece.shape[0]
    per = half // shards
    core = axes.bit(axes.core)
    owner = 1 - core if other else core
    slot = axes.slot(stream, owner)
    copies = []
    for index in range(shards):
        spot = pl.multiple_of(owner * half + (index ^ slot) * per, per)
        rows = slice(index * per, (index + 1) * per)
        first = 0
        for part, (out, buffer, width) in enumerate(zip(outs, wide, splits)):
            buffer[rows, :] = piece[rows, first : first + width].astype(f32)
            first += width
            copy = pltpu.make_async_copy(
                buffer.at[rows, :], out.at[pl.ds(spot, per), :], sems.at[index, part]
            )
            copy.start()
            copies.append(copy)
    for copy in copies:
        copy.wait()


def spread_half(axes, stream, shards, splits, piece, outs=None):
    half = piece.shape[0]
    hbm = pl.BlockSpec(memory_space=pltpu.HBM)
    other = outs is not None
    return pl.pallas_call(
        functools.partial(spread_kernel, axes, stream, shards, splits, other),
        out_shape=[jax.ShapeDtypeStruct((2 * half, width), f32) for width in splits],
        in_specs=[pl.BlockSpec(memory_space=pltpu.VMEM)] + ([hbm] * len(splits) if other else []),
        out_specs=[hbm] * len(splits),
        scratch_shapes=[pltpu.VMEM((half, width), f32) for width in splits]
        + [pltpu.SemaphoreType.DMA((shards, len(splits)))],
        input_output_aliases={1 + index: index for index in range(len(splits))} if other else {},
        compiler_params=pltpu.CompilerParams(vmem_limit_bytes=8 * MIB),
    )(piece, *(outs or ()))


def on_device(kernel, operands, outs, scratch=(), sems=()):
    buffers = [pltpu.VMEM(value.shape, value.dtype) for value in operands]
    buffers += [pltpu.VMEM(shape, dtype) for shape, dtype in outs]
    hbm = pl.BlockSpec(memory_space=pltpu.HBM)
    return pl.pallas_call(
        kernel,
        out_shape=[jax.ShapeDtypeStruct(shape, dtype) for shape, dtype in outs],
        in_specs=[hbm] * len(operands),
        out_specs=[hbm] * len(outs),
        scratch_shapes=buffers
        + [pltpu.VMEM(shape, dtype) for shape, dtype in scratch]
        + [pltpu.SemaphoreType.DMA(shape) for shape in sems],
        compiler_params=pltpu.CompilerParams(vmem_limit_bytes=60 * MIB),
    )(*operands)


class Axes:
    def __init__(self, mesh):
        self.sizes = dict(mesh.shape)
        bits = self.sizes["items"].bit_length() - 1
        self.core = ("lat", 1)
        named = {"x": ("lat", 2), "y": ("items", 1), "z": ("items", 2), "w": ("items", 4)}
        self.orders = [[[named[key] for key in order] for order in pair] for pair in ORDERS]
        self.extra = [("items", 1 << bit) for bit in range(3, bits)]

    def bit(self, dim):
        axis, value = dim
        return (lax.axis_index(axis) // value) % 2

    def slot(self, stream, core):
        pair = []
        for order in self.orders[stream]:
            total = 0
            for dim in order[:-1]:
                total = total * 2 + self.bit(dim)
            pair.append(total)
        return jnp.where(core == 0, pair[0], pair[1])

    def has_below(self):
        return lax.axis_index("lat") > 0

    def has_above(self):
        return lax.axis_index("lat") < self.sizes["lat"] - 1

    def beside(self, value):
        return self.exchange(value, (self.core, self.core))

    def across(self, value):
        count = self.sizes["lat"]
        pairs = [(index, (index + 1) // 2 * 4 - 1 - index) for index in range(1, count - 1)]
        return lax.ppermute(value, "lat", pairs)

    def exchange(self, value, dims):
        items = self.sizes["items"]
        pairs = []
        for index in range(self.sizes["lat"] * items):
            axis, bit = dims[index // items % 2]
            pairs.append((index, index ^ (bit * items if axis == "lat" else bit)))
        return lax.ppermute(value, ("lat", "items"), pairs)


def add_rows(terms, low, high):
    total = terms[0][low:high].astype(f32)
    for term in terms[1:]:
        total = total + term[low:high].astype(f32)
    return total


def sum_stream(axes, stream, keep, send, half_done, small=None, small_done=None):
    core = (axes.core, axes.core)
    terms = [keep, (yield send, core)]
    rows = keep.shape[0]
    extra = 0 if small is None else small.shape[0]
    pairs = list(zip(*axes.orders[stream]))
    hops, whole = pairs[:-1], pairs[-1:] + [(dim, dim) for dim in axes.extra]
    for dims in hops:
        rows //= 2
        value = add_rows(terms, rows, 2 * rows).astype(bf16)
        if extra:
            value = jnp.concatenate([value, small], axis=0)
        got = yield value, dims
        if extra:
            small = (small.astype(f32) + got[rows:].astype(f32)).astype(bf16)
        terms.append(got)
    piece = add_rows(terms, 0, rows).astype(bf16)
    for dims in whole:
        value = jnp.concatenate([piece, small], axis=0) if extra else piece
        got = yield value, dims
        if extra:
            small = (small.astype(f32) + got[rows:].astype(f32)).astype(bf16)
        piece = (piece.astype(f32) + got[:rows].astype(f32)).astype(bf16)
    if extra:
        got = yield small, core
        small_done(small.astype(f32) + got.astype(f32))
    for dims in reversed(hops):
        got = yield piece, dims
        piece = jnp.concatenate([piece, got], axis=0)
    half_done(piece)
    return (yield piece, core)


def after(value, token):
    if token is None:
        return value
    return lax.optimization_barrier((value, token))[0]


class Sequence:
    def __init__(self, axes):
        self.axes = axes
        self.token = None
        self.waiting = {}
        self.streams = {}
        self.done = {}
        self.count = {}
        self.then = None
        self.held = None

    def add(self, name, stream):
        self.streams[name] = stream
        self.waiting[name] = None

    def step(self, name):
        got = self.waiting[name]
        try:
            value, dims = self.streams[name].send(None if got is None else after(got, self.token))
        except StopIteration as end:
            self.done[name] = end.value
            return
        if self.held is not None:
            value = after(value, self.held)
            self.held = None
        self.token = value
        self.count[name] = self.count.get(name, -1) + 1
        with jax.named_scope(f"s{name}h{self.count[name]}"):
            self.waiting[name] = self.axes.exchange(value, dims)
        if self.then is not None:
            act, self.then = self.then, None
            act()

    def steps(self, names):
        for name in names:
            if name not in self.done:
                self.step(name)


def body(
    axes,
    tokens,
    norm1_gain,
    norm1_bias,
    qkv_weight,
    qv_bias,
    proj_weight,
    proj_bias,
    norm2_gain,
    norm2_bias,
    fc1_weight,
    fc1_bias,
    fc2_weight,
    fc2_bias,
    cotangent,
):
    items, steps, lat_dev, lon, width = tokens.shape
    hidden = fc1_weight.shape[1]
    rows = items * steps * lat_dev * lon
    side = items * steps * lon
    lat_total = axes.sizes["lat"]
    shards = 8
    odd = axes.bit(axes.core) == 1
    first = tokens[:, :, 0].reshape(side, width)
    last = tokens[:, :, lat_dev - 1].reshape(side, width)
    beside = axes.beside(jnp.where(odd, first, last))
    across = axes.across(jnp.where(odd, last, first))
    flat_tokens = tokens.reshape(rows, width)
    flat_cot = cotangent.reshape(rows, width)
    operands = (
        flat_tokens,
        norm1_gain,
        norm1_bias,
        qv_bias,
        beside,
        across,
        qkv_weight,
        proj_weight,
        proj_bias,
        norm2_gain,
        norm2_bias,
        fc1_weight,
        fc1_bias,
        fc2_weight,
        fc2_bias,
        flat_cot,
    )
    band = rows // items
    keys = band + 2 * side // items
    groups = width // 128
    both = hidden + width
    (mixed, a_low, dx1, small, keep1, send1, keep2, send2, dq, dk, dv, to_beside, to_across) = on_device(
        functools.partial(block_kernel, axes, shards, items, steps, lat_dev, lon),
        operands,
        [
            ((rows, width), bf16),
            ((rows, width), bf16),
            ((rows, width), f32),
            ((4 + hidden // width, width), f32),
            ((hidden // 2, width), bf16),
            ((hidden // 2, width), bf16),
            ((width // 2, both), bf16),
            ((width // 2, both), bf16),
            ((rows, width), bf16),
            ((rows, width), f32),
            ((rows, width), f32),
            ((2, side, width), bf16),
            ((2, side, width), bf16),
        ],
        scratch=[
            ((2, rows + 2 * side, width), bf16),
            ((rows, width), bf16),
            ((items * groups, GROUP * band, keys), f32),
            ((rows, width), bf16),
            ((rows, width), bf16),
            ((rows, width), bf16),
            ((rows, hidden), bf16),
            ((rows, hidden), bf16),
            ((rows, width), bf16),
        ],
        sems=[(16,), (13, items)],
    )

    from_beside = axes.beside(to_beside)
    from_across = axes.across(to_across)
    grads = {}
    splits = {1: (width,), 2: (hidden, width), 3: (3 * width,)}

    def half_done(name):
        def act(piece):
            def run():
                held = after(piece, sequence.token)
                grads[name] = spread_half(axes, name - 1, shards, splits[name], held)
                sequence.token = grads[name][0]

            sequence.then = run

        return act

    def small_done(total):
        total = total.reshape(8 + hidden // width, width)
        grads["small"] = (
            total[0],
            total[1],
            total[2:4],
            total[7],
            total[4],
            total[5],
            total[8:].reshape(hidden),
            total[6],
        )
        sequence.held = grads["small"]

    sequence = Sequence(axes)
    sequence.token = (to_beside, to_across)
    sequence.add(1, sum_stream(axes, 0, keep1, send1, half_done(1)))
    sequence.add(2, sum_stream(axes, 1, keep2, send2, half_done(2)))
    sequence.steps((2, 1))
    sequence.token = (from_beside, from_across)
    def join():
        operands = (
            after(dq, sequence.token),
            dk,
            dv,
            from_beside,
            from_across,
            a_low,
            qkv_weight,
            flat_tokens,
            norm1_gain,
            dx1,
            small,
        )
        keep, send, grad, sums = on_device(
            functools.partial(qkv_grad_kernel, axes, shards, lat_dev, lon),
            operands,
            [
                ((width // 2, 3 * width), bf16),
                ((width // 2, 3 * width), bf16),
                ((rows, width), bf16),
                (((8 + hidden // width) // 3, 3 * width), bf16),
            ],
            scratch=[((rows, 3 * width), bf16)],
            sems=[(11,), (4,)],
        )
        sequence.add(3, sum_stream(axes, 2, keep, send, half_done(3), sums, small_done))
        return grad

    for name in ORDER + (1, 2, 3) * 12:
        if name in sequence.done:
            continue
        if name == 3 and 3 not in sequence.streams:
            tokens_grad = join()
        sequence.step(name)
        if name in sequence.done:
            other = after(sequence.done[name], sequence.token)
            grads[name] = spread_half(axes, name - 1, shards, splits[name], other, grads[name])
            sequence.token = grads[name][0]
    (grad_fc2,) = grads[1]
    grad_fc1, grad_proj = grads[2]
    (grad_qkv,) = grads[3]
    sums = grads["small"]
    return (
        mixed.reshape(tokens.shape),
        tokens_grad.reshape(tokens.shape),
        sums[0],
        sums[1],
        grad_qkv,
        sums[2],
        grad_proj,
        sums[3],
        sums[4],
        sums[5],
        grad_fc1,
        sums[6],
        grad_fc2,
        sums[7],
    )


def solution(mesh):
    split = P("items", None, "lat", None, None)
    whole = P()
    return jax.shard_map(
        functools.partial(body, Axes(mesh)),
        mesh=mesh,
        in_specs=(split,) + (whole,) * 12 + (split,),
        out_specs=(split, split) + (whole,) * 12,
        check_vma=False,
    )
```

```python
import functools
import math

import jax
import jax.numpy as jnp
from jax import lax
from jax.experimental import pallas as pl
from jax.experimental.pallas import tpu as pltpu
from jax.sharding import PartitionSpec as P

HEAD_DIM = 32
ROW_REACH = 1
COL_REACH = 2
GROUP = 128 // HEAD_DIM
EPSILON = 1e-06
SCALE = HEAD_DIM ** (-0.5)
SQRT_HALF = 0.5**0.5
PHI_SCALE = (2.0 * math.pi) ** (-0.5)
NEGATIVE = -1e30
ORDERS = (("zxyw", "xyzw"), ("yzxw", "zywx"), ("yxwz", "xywz"))
ORDER = (2, 3, 1, 3, 2, 1, 3, 2, 1, 3, 2, 1, 3, 2, 1, 2, 3, 1, 2, 3, 1, 3, 2, 1, 3, 2, 1, 3)

f32 = jnp.float32
bf16 = jnp.bfloat16
MIB = 1024 * 1024


def dot_nn(left, right):
    return lax.dot_general(left, right, (((1,), (0,)), ((), ())), preferred_element_type=f32)


def dot_nt(left, right):
    return lax.dot_general(left, right, (((1,), (1,)), ((), ())), preferred_element_type=f32)


def dot_tn(left, right):
    return lax.dot_general(left, right, (((0,), (0,)), ((), ())), preferred_element_type=f32)


def normed(values):
    mean = jnp.mean(values, axis=-1, keepdims=True)
    centred = values - mean
    spread = jnp.mean(centred * centred, axis=-1, keepdims=True)
    scale = lax.rsqrt(spread + EPSILON)
    return centred * scale, scale


def norm_back(grad, gain, unit, scale):
    scaled = grad * gain
    first = jnp.mean(scaled, axis=-1, keepdims=True)
    second = jnp.mean(scaled * unit, axis=-1, keepdims=True)
    return scale * (scaled - first - unit * second)


def as_row(ref):
    return ref[...].astype(f32).reshape(1, ref.shape[0])


def stack_heads(block, lane_head):
    zero = jnp.zeros_like(block)
    return jnp.concatenate(
        [jnp.where(lane_head == head, block, zero) for head in range(GROUP)], axis=0
    )


def fold_heads(stacked, lane_head, rows):
    total = jnp.where(lane_head == 0, stacked[:rows], 0.0)
    for head in range(1, GROUP):
        total = jnp.where(lane_head == head, stacked[head * rows : (head + 1) * rows], total)
    return total


def window_bias(axes, steps, lat_dev, lon):
    band = steps * lat_dev * lon
    keys = band + 2 * steps * lon
    query = lax.broadcasted_iota(jnp.int32, (band, keys), 0)
    key = lax.broadcasted_iota(jnp.int32, (band, keys), 1)
    query_row = query // lon % lat_dev
    first = jnp.where(axes.has_below(), -1, -2 - ROW_REACH)
    last = jnp.where(axes.has_above(), lat_dev, lat_dev + 1 + ROW_REACH)
    key_row = jnp.where(
        key < band, key // lon % lat_dev, jnp.where(key < band + steps * lon, first, last)
    )
    gap = jnp.abs(query % lon - key % lon)
    gap = jnp.minimum(gap, lon - gap)
    seen = (jnp.abs(query_row - key_row) <= ROW_REACH) & (gap <= COL_REACH)
    return jnp.where(seen, 0.0, NEGATIVE)


def block_kernel(
    axes,
    shards,
    items,
    steps,
    lat_dev,
    lon,
    *refs,
):
    sources, finals, refs = refs[:16], refs[16:29], refs[29:]
    targets, locals_, refs = refs[:16], refs[16:29], refs[29:]
    kv_ref, q_ref, p_ref, do_ref, o_ref, c_ref, g_ref, du_ref, dy_ref, in_sems, out_sems = refs
    fetches = start_copies(sources, targets, in_sems)
    (tok, gain1, bias1, qv_bias, beside, across, wqkv, wproj) = targets[:8]
    (bproj, gain2, bias2, w1, b1, w2, b2, cot) = targets[8:]
    (mixed_out, a_out, dx1_out, small_out, keep1, send1, keep2, send2) = locals_[:8]
    (dq_out, dk_out, dv_out, to_beside, to_across) = locals_[8:]
    leaving = []

    def leave(index, slot=0, window=None):
        source, target = locals_[index], finals[index]
        if window is not None:
            source, target = source.at[window], target.at[window]
        copy = pltpu.make_async_copy(source, target, out_sems.at[index, slot])
        copy.start()
        leaving.append(copy)

    for copy in fetches[:6]:
        copy.wait()
    rows, width = tok.shape
    hidden = w1.shape[1]
    side = beside.shape[0]
    band = rows // items
    edge = side // items
    groups = width // 128
    lane_head = lax.broadcasted_iota(jnp.int32, (1, 128), 1) // HEAD_DIM

    g1 = as_row(gain1)
    h1 = as_row(bias1)
    x = tok[...].astype(f32)
    unit, _ = normed(x)
    a_own = (unit * g1 + h1).astype(bf16)
    a_out[...] = a_own
    leave(1)
    wide = jnp.concatenate([beside[...], across[...]], axis=0).astype(f32)
    unit_wide, _ = normed(wide)
    a_wide = (unit_wide * g1 + h1).astype(bf16)
    a_all = jnp.concatenate([a_own, a_wide], axis=0)
    fetches[6].wait()
    q_ref[...] = (dot_nn(a_own, wqkv[:, :width]) + qv_bias[0:1, :].astype(f32)).astype(bf16)
    kv_ref[0] = dot_nn(a_all, wqkv[:, width : 2 * width]).astype(bf16)
    kv_ref[1] = (dot_nn(a_all, wqkv[:, 2 * width :]) + qv_bias[1:2, :].astype(f32)).astype(bf16)

    window = jnp.concatenate([window_bias(axes, steps, lat_dev, lon)] * GROUP, axis=0)
    odd = axes.bit(axes.core)
    below = pl.multiple_of(rows + (1 - odd) * side, 16)
    above = pl.multiple_of(rows + odd * side, 16)

    def keys_of(which, item, lanes):
        return jnp.concatenate(
            [
                kv_ref[which, item * band : (item + 1) * band, lanes],
                kv_ref[which, pl.ds(below + item * edge, edge), lanes],
                kv_ref[which, pl.ds(above + item * edge, edge), lanes],
            ],
            axis=0,
        )

    for item in range(items):
        for group in range(groups):
            lanes = slice(group * 128, (group + 1) * 128)
            own = slice(item * band, (item + 1) * band)
            queries = stack_heads(q_ref[own, lanes], lane_head)
            scores = dot_nt(queries, keys_of(0, item, lanes)) * SCALE + window
            top = jnp.max(scores, axis=-1, keepdims=True)
            weights = jnp.exp(scores - top)
            total = jnp.sum(weights, axis=-1, keepdims=True)
            soft = weights * (1.0 / total)
            p_ref[item * groups + group] = soft
            mixed_heads = dot_nn(soft.astype(bf16), keys_of(1, item, lanes))
            o_ref[own, lanes] = fold_heads(mixed_heads, lane_head, band).astype(bf16)

    for copy in fetches[7:]:
        copy.wait()
    g2 = as_row(gain2)
    h2 = as_row(bias2)
    x1 = x + dot_nn(o_ref[...], wproj[...]) + as_row(bproj)
    unit2, scale2 = normed(x1)
    c_low = (unit2 * g2 + h2).astype(bf16)
    c_ref[...] = c_low
    cot_low = cot[...]
    branch = jnp.zeros((rows, width), f32)
    dc = jnp.zeros((rows, width), f32)
    b1_row = as_row(b1)
    for part in range(hidden // width):
        cols = slice(part * width, (part + 1) * width)
        u = dot_nn(c_low, w1[:, cols]) + b1_row[:, cols]
        cdf = 0.5 + 0.5 * lax.erf(u * SQRT_HALF)
        slope = cdf + u * (jnp.exp(u * u * -0.5) * PHI_SCALE)
        act = (u * cdf).astype(bf16)
        g_ref[:, cols] = act
        branch = branch + dot_nn(act, w2[cols, :])
        dh = dot_nt(cot_low, w2[cols, :])
        du_low = (dh * slope).astype(bf16)
        du_ref[:, cols] = du_low
        small_out[4 + part : 5 + part, :] = jnp.sum(du_low.astype(f32), axis=0, keepdims=True)
        dc = dc + dot_nt(du_low, w1[:, cols])
    mixed_out[...] = (x1 + branch + as_row(b2)).astype(bf16)
    cot_wide = cot_low.astype(f32)
    small_out[0:1, :] = jnp.sum(dc * unit2, axis=0, keepdims=True)
    small_out[1:2, :] = jnp.sum(dc, axis=0, keepdims=True)
    small_out[2:3, :] = jnp.sum(cot_wide, axis=0, keepdims=True)
    dx1 = cot_wide + norm_back(dc, g2, unit2, scale2)
    dx1_out[...] = dx1
    leave(0)
    leave(2)
    dy = dx1.astype(bf16)
    dy_ref[...] = dy
    small_out[3:4, :] = jnp.sum(dy.astype(f32), axis=0, keepdims=True)
    do_ref[...] = dot_nt(dy, wproj[...]).astype(bf16)
    leave(3)
    grad_halves(axes, 0, shards, g_ref, cot, keep1, send1)
    leave(4)
    leave(5)
    grad_halves(axes, 1, shards, c_ref, du_ref, keep2, send2, slice(0, hidden))
    grad_halves(axes, 1, shards, o_ref, dy_ref, keep2, send2, slice(hidden, hidden + width))
    leave(6)
    leave(7)

    for item in range(items):
        for group in range(groups):
            lanes = slice(group * 128, (group + 1) * 128)
            own = slice(item * band, (item + 1) * band)
            ends = slice(item * edge, (item + 1) * edge)
            grads = stack_heads(do_ref[own, lanes], lane_head)
            queries = stack_heads(q_ref[own, lanes], lane_head)
            soft = p_ref[item * groups + group]
            dp = dot_nt(grads, keys_of(1, item, lanes))
            inner = jnp.sum(soft * dp, axis=-1, keepdims=True)
            ds = (soft * (dp - inner)).astype(bf16)
            dq = fold_heads(dot_nn(ds, keys_of(0, item, lanes)), lane_head, band) * SCALE
            dq_out[own, lanes] = dq.astype(bf16)
            dk = dot_tn(ds, queries) * SCALE
            dv = dot_tn(soft.astype(bf16), grads)
            dk_out[own, lanes] = dk[:band]
            dv_out[own, lanes] = dv[:band]
            for index, grad in ((0, dk), (1, dv)):
                down = grad[band : band + edge]
                up = grad[band + edge :]
                to_beside[index, ends, lanes] = jnp.where(odd == 1, down, up).astype(bf16)
                to_across[index, ends, lanes] = jnp.where(odd == 1, up, down).astype(bf16)
        for index in (8, 9, 10):
            leave(index, item, (own, slice(None)))
        for index in (11, 12):
            leave(index, item, (slice(None), ends, slice(None)))
    for copy in leaving:
        copy.wait()


def start_copies(sources, targets, sems, first=0):
    copies = [
        pltpu.make_async_copy(source, target, sems.at[first + index])
        for index, (source, target) in enumerate(zip(sources, targets))
    ]
    for copy in copies:
        copy.start()
    return copies


def grad_halves(axes, stream, shards, left, right, keep, send, lanes=slice(None)):
    half = left.shape[1] // 2
    per = half // shards
    step = min(half, 256)
    core = axes.bit(axes.core)
    values = right[...]
    for ref, owner in ((keep, core), (send, 1 - core)):
        slot = axes.slot(stream, owner)
        for start in range(0, half, step):
            columns = pl.ds(pl.multiple_of(owner * half + start, 128), step)
            product = dot_tn(left[:, columns], values)
            for index in range(step // per):
                spot = pl.multiple_of(((start // per + index) ^ slot) * per, per)
                ref[pl.ds(spot, per), lanes] = product[index * per : (index + 1) * per].astype(bf16)


def qkv_grad_kernel(
    axes,
    shards,
    lat_dev,
    lon,
    *refs,
):
    sources, finals, refs = refs[:11], refs[11:15], refs[15:]
    targets, locals_, refs = refs[:11], refs[11:15], refs[15:]
    joined, in_sems, out_sems = refs
    fetches = start_copies(sources, targets, in_sems)
    dq, dk, dv, from_beside, from_across, a_low, wqkv, tok, gain1, dx1, small_in = targets
    keep, send, tokens_out, small_out = locals_
    for copy in fetches[:6]:
        copy.wait()
    rows, width = tok.shape
    joined[:, :width] = dq[...]
    odd = axes.bit(axes.core) == 1
    for which, grads in ((0, dk), (1, dv)):
        columns = slice((1 + which) * width, (2 + which) * width)
        for strip in range(rows // (lat_dev * lon)):
            edge = slice(strip * lon, (strip + 1) * lon)
            for row in range(lat_dev):
                start = (strip * lat_dev + row) * lon
                value = grads[start : start + lon, :]
                near = from_beside[which, edge, :].astype(f32)
                far = from_across[which, edge, :].astype(f32)
                if row == 0:
                    value = value + jnp.where(odd, near, far)
                if row == lat_dev - 1:
                    value = value + jnp.where(odd, far, near)
                joined[start : start + lon, columns] = value.astype(bf16)
    grad_halves(axes, 2, shards, a_low, joined, keep, send)
    leaving = start_copies(locals_[:2], finals[:2], out_sems)
    for copy in fetches[6:]:
        copy.wait()
    da = dot_nt(joined[...], wqkv[...])
    unit, scale = normed(tok[...].astype(f32))
    grad = dx1[...] + norm_back(da, as_row(gain1), unit, scale)
    tokens_out[...] = grad.astype(bf16)
    sums = [
        jnp.sum(da * unit, axis=0, keepdims=True),
        jnp.sum(da, axis=0, keepdims=True),
        jnp.sum(joined[:, :width].astype(f32), axis=0, keepdims=True),
        jnp.sum(joined[:, 2 * width :].astype(f32), axis=0, keepdims=True),
    ] + [small_in[index : index + 1, :] for index in range(small_in.shape[0])]
    for index, row in enumerate(sums):
        place_of = slice(index % 3 * width, (index % 3 + 1) * width)
        small_out[index // 3 : index // 3 + 1, place_of] = row.astype(bf16)
    leaving += start_copies(locals_[2:], finals[2:], out_sems, 2)
    for copy in leaving:
        copy.wait()


def spread_kernel(axes, stream, shards, splits, other, sums, *refs):
    count = len(splits)
    piece = refs[0]
    outs = refs[-2 * (count + len(sums)) - 1 : -count - len(sums) - 1]
    wide, sems = refs[-count - len(sums) - 1 : -1], refs[-1]
    core = axes.bit(axes.core)
    owner = 1 - core if other else core
    slot = axes.slot(stream, owner)
    per = outs[0].shape[0] // (2 * shards)
    copies = []

    def leave(source, target, index, part):
        copy = pltpu.make_async_copy(source, target, sems.at[index, part])
        copy.start()
        copies.append(copy)

    for index in range(shards):
        spot = pl.multiple_of((owner * shards + (index ^ slot)) * per, per)
        rows = slice(index * per, (index + 1) * per)
        first = 0
        for part, width in enumerate(splits):
            wide[part][rows, :] = piece[rows, first : first + width].astype(f32)
            first += width
            leave(wide[part].at[rows, :], outs[part].at[pl.ds(spot, per), :], index, part)
    if sums:
        rows = slice(shards * per, piece.shape[0])
        total = refs[1][rows, :].astype(f32) + piece[rows, :].astype(f32)
        width = total.shape[1] // 3
        taken = [total[k // 3 : k // 3 + 1, k % 3 * width : (k % 3 + 1) * width] for k in range(3 * total.shape[0])]
        for part, (first, shape) in enumerate(sums):
            buffer = wide[count + part]
            for k in range(math.prod(shape) // width):
                if len(shape) == 1:
                    buffer[k * width : (k + 1) * width] = taken[first + k].reshape(width)
                else:
                    buffer[k : k + 1, :] = taken[first + k]
            leave(buffer, outs[count + part], part, count)
    for copy in copies:
        copy.wait()


def spread(axes, stream, shards, splits, rows, pieces, outs=(), sums=()):
    held = rows // 2
    hbm = pl.BlockSpec(memory_space=pltpu.HBM)
    shapes = [(rows, width) for width in splits] + [shape for _, shape in sums]
    return pl.pallas_call(
        functools.partial(spread_kernel, axes, stream, shards, splits, bool(outs), sums),
        out_shape=[jax.ShapeDtypeStruct(shape, f32) for shape in shapes],
        in_specs=[pl.BlockSpec(memory_space=pltpu.VMEM)] * len(pieces) + [hbm] * len(outs),
        out_specs=[hbm] * len(shapes),
        scratch_shapes=[pltpu.VMEM((held, width), f32) for width in splits]
        + [pltpu.VMEM(shape, f32) for _, shape in sums]
        + [pltpu.SemaphoreType.DMA((max(shards, len(sums)), len(splits) + 1))],
        input_output_aliases={len(pieces) + index: index for index in range(len(outs))},
        compiler_params=pltpu.CompilerParams(vmem_limit_bytes=8 * MIB),
        cost_estimate=pl.CostEstimate(
            flops=0, bytes_accessed=6 * held * sum(splits), transcendentals=0
        ),
    )(*pieces, *outs)


def on_device(kernel, operands, outs, scratch=(), sems=(), flops=0):
    buffers = [pltpu.VMEM(value.shape, value.dtype) for value in operands]
    buffers += [pltpu.VMEM(shape, jnp.dtype(dtype)) for shape, dtype in outs]
    hbm = pl.BlockSpec(memory_space=pltpu.HBM)
    return pl.pallas_call(
        kernel,
        out_shape=[jax.ShapeDtypeStruct(shape, dtype) for shape, dtype in outs],
        in_specs=[hbm] * len(operands),
        out_specs=[hbm] * len(outs),
        scratch_shapes=buffers
        + [pltpu.VMEM(shape, dtype) for shape, dtype in scratch]
        + [pltpu.SemaphoreType.DMA(shape) for shape in sems],
        compiler_params=pltpu.CompilerParams(vmem_limit_bytes=60 * MIB),
        cost_estimate=pl.CostEstimate(
            flops=flops,
            bytes_accessed=sum(math.prod(buffer.shape) * buffer.dtype.itemsize for buffer in buffers),
            transcendentals=0,
        ),
    )(*operands)


class Axes:
    def __init__(self, mesh):
        self.sizes = dict(mesh.shape)
        bits = self.sizes["items"].bit_length() - 1
        self.core = ("lat", 1)
        named = {"x": ("lat", 2), "y": ("items", 1), "z": ("items", 2), "w": ("items", 4)}
        self.orders = [[[named[key] for key in order] for order in pair] for pair in ORDERS]
        self.extra = [("items", 1 << bit) for bit in range(3, bits)]

    def bit(self, dim):
        axis, value = dim
        return (lax.axis_index(axis) // value) % 2

    def slot(self, stream, core):
        pair = []
        for order in self.orders[stream]:
            total = 0
            for dim in order[:-1]:
                total = total * 2 + self.bit(dim)
            pair.append(total)
        return jnp.where(core == 0, pair[0], pair[1])

    def has_below(self):
        return lax.axis_index("lat") > 0

    def has_above(self):
        return lax.axis_index("lat") < self.sizes["lat"] - 1

    def beside(self, value):
        return self.exchange(value, (self.core, self.core))

    def across(self, value):
        count = self.sizes["lat"]
        pairs = [(index, (index + 1) // 2 * 4 - 1 - index) for index in range(1, count - 1)]
        return lax.ppermute(value, "lat", pairs)

    def exchange(self, value, dims):
        items = self.sizes["items"]
        pairs = []
        for index in range(self.sizes["lat"] * items):
            axis, bit = dims[index // items % 2]
            pairs.append((index, index ^ (bit * items if axis == "lat" else bit)))
        return lax.ppermute(value, ("lat", "items"), pairs)


def add_rows(terms, low, high):
    total = terms[0][low:high].astype(f32)
    for term in terms[1:]:
        total = total + term[low:high].astype(f32)
    return total


def after(value, token):
    return lax.optimization_barrier((value, token))[0]


class Sequence:
    def __init__(self, axes, token):
        self.axes = axes
        self.token = token

    def ready(self, value):
        return after(value, self.token)

    def swap(self, value, dims, scope="swap"):
        self.token = value
        with jax.named_scope(scope):
            return self.axes.exchange(value, dims)


def sum_stream(sequence, stream, keep, send, write, small=None):
    axes = sequence.axes
    core = (axes.core, axes.core)
    label = (f"s{stream + 1}h{hop}" for hop in range(99))
    got = sequence.swap(send, core, next(label))
    yield
    terms = [keep, sequence.ready(got)]
    rows = keep.shape[0]
    extra = 0 if small is None else small.shape[0]
    pairs = list(zip(*axes.orders[stream]))
    hops, whole = pairs[:-1], pairs[-1:] + [(dim, dim) for dim in axes.extra]
    for dims in hops:
        rows //= 2
        value = add_rows(terms, rows, 2 * rows).astype(bf16)
        if extra:
            value = jnp.concatenate([value, small], axis=0)
        got = sequence.swap(value, dims, next(label))
        yield
        got = sequence.ready(got)
        if extra:
            small = (small.astype(f32) + got[rows:].astype(f32)).astype(bf16)
        terms.append(got)
    piece = add_rows(terms, 0, rows).astype(bf16)
    for dims in whole:
        value = jnp.concatenate([piece, small], axis=0) if extra else piece
        got = sequence.swap(value, dims, next(label))
        yield
        got = sequence.ready(got)
        if extra:
            small = (small.astype(f32) + got[rows:].astype(f32)).astype(bf16)
        piece = (piece.astype(f32) + got[:rows].astype(f32)).astype(bf16)
    for dims in reversed(hops):
        got = sequence.swap(piece, dims, next(label))
        yield
        parts = [piece, sequence.ready(got)]
        if extra and dims is hops[0]:
            parts.append(small)
        piece = jnp.concatenate(parts, axis=0)
    near = sequence.swap(piece, core, next(label))
    write(piece)
    yield
    write(piece, sequence.ready(near))


def body(
    axes,
    tokens,
    norm1_gain,
    norm1_bias,
    qkv_weight,
    qv_bias,
    proj_weight,
    proj_bias,
    norm2_gain,
    norm2_bias,
    fc1_weight,
    fc1_bias,
    fc2_weight,
    fc2_bias,
    cotangent,
):
    items, steps, lat_dev, lon, width = tokens.shape
    hidden = fc1_weight.shape[1]
    rows = items * steps * lat_dev * lon
    side = items * steps * lon
    lat_total = axes.sizes["lat"]
    shards = 8
    odd = axes.bit(axes.core) == 1
    first = tokens[:, :, 0].reshape(side, width)
    last = tokens[:, :, lat_dev - 1].reshape(side, width)
    beside = axes.beside(jnp.where(odd, first, last))
    across = axes.across(jnp.where(odd, last, first))
    flat_tokens = tokens.reshape(rows, width)
    flat_cot = cotangent.reshape(rows, width)
    operands = (
        flat_tokens,
        norm1_gain,
        norm1_bias,
        qv_bias,
        beside,
        across,
        qkv_weight,
        proj_weight,
        proj_bias,
        norm2_gain,
        norm2_bias,
        fc1_weight,
        fc1_bias,
        fc2_weight,
        fc2_bias,
        flat_cot,
    )
    band = rows // items
    keys = band + 2 * side // items
    groups = width // 128
    both = hidden + width
    (mixed, a_low, dx1, small, keep1, send1, keep2, send2, dq, dk, dv, to_beside, to_across) = on_device(
        functools.partial(block_kernel, axes, shards, items, steps, lat_dev, lon),
        operands,
        [
            ((rows, width), bf16),
            ((rows, width), bf16),
            ((rows, width), f32),
            ((4 + hidden // width, width), f32),
            ((hidden // 2, width), bf16),
            ((hidden // 2, width), bf16),
            ((width // 2, both), bf16),
            ((width // 2, both), bf16),
            ((rows, width), bf16),
            ((rows, width), f32),
            ((rows, width), f32),
            ((2, side, width), bf16),
            ((2, side, width), bf16),
        ],
        scratch=[
            ((2, rows + 2 * side, width), bf16),
            ((rows, width), bf16),
            ((items * groups, GROUP * band, keys), f32),
            ((rows, width), bf16),
            ((rows, width), bf16),
            ((rows, width), bf16),
            ((rows, hidden), bf16),
            ((rows, hidden), bf16),
            ((rows, width), bf16),
        ],
        sems=[(16,), (13, items)],
        flops=2 * rows * width * (4 * width + 6 * hidden),
    )

    from_beside = axes.beside(to_beside)
    from_across = axes.across(to_across)
    sequence = Sequence(axes, (to_beside, to_across))
    grads = {}
    splits = {1: (width,), 2: (hidden, width), 3: (3 * width,)}

    def stream(name, keep, send, small=None):
        rows = 2 * keep.shape[0]
        settings = (axes, name - 1, shards, splits[name], rows)

        def write(own, other=None):
            if other is None:
                grads[name] = spread(*settings, (own,))
            elif small is None:
                grads[name] = spread(*settings, (other,), grads[name])
            else:
                grads[name] = spread(*settings, (other, own), grads[name], small_places)
            sequence.token = grads[name][0]

        return sum_stream(sequence, name - 1, keep, send, write, small)

    small_places = (
        (0, (width,)),
        (1, (width,)),
        (2, (2, width)),
        (7, (width,)),
        (4, (width,)),
        (5, (width,)),
        (8, (hidden,)),
        (6, (width,)),
    )
    streams = {1: stream(1, keep1, send1), 2: stream(2, keep2, send2)}
    next(streams[2])
    next(streams[1])
    sequence.token = from_beside

    def join():
        operands = (
            after(dq, sequence.token),
            dk,
            dv,
            from_beside,
            from_across,
            a_low,
            qkv_weight,
            flat_tokens,
            norm1_gain,
            dx1,
            small,
        )
        keep, send, grad, sums = on_device(
            functools.partial(qkv_grad_kernel, axes, shards, lat_dev, lon),
            operands,
            [
                ((width // 2, 3 * width), bf16),
                ((width // 2, 3 * width), bf16),
                ((rows, width), bf16),
                (((8 + hidden // width) // 3, 3 * width), bf16),
            ],
            scratch=[((rows, 3 * width), bf16)],
            sems=[(11,), (4,)],
            flops=12 * rows * width * width,
        )
        streams[3] = stream(3, keep, send, sums)
        return grad

    for name in ORDER + (1, 2, 3) * 12:
        if name not in streams:
            tokens_grad = join()
        next(streams[name], None)
    (grad_fc2,) = grads[1]
    grad_fc1, grad_proj = grads[2]
    grad_qkv, *sums = grads[3]
    return (
        mixed.reshape(tokens.shape),
        tokens_grad.reshape(tokens.shape),
        sums[0],
        sums[1],
        grad_qkv,
        sums[2],
        grad_proj,
        sums[3],
        sums[4],
        sums[5],
        grad_fc1,
        sums[6],
        grad_fc2,
        sums[7],
    )


def solution(mesh):
    split = P("items", None, "lat", None, None)
    whole = P()
    return jax.shard_map(
        functools.partial(body, Axes(mesh)),
        mesh=mesh,
        in_specs=(split,) + (whole,) * 12 + (split,),
        out_specs=(split, split) + (whole,) * 12,
        check_vma=False,
    )
```

```python
import functools
import math

import jax
import jax.numpy as jnp
from jax import lax
from jax.experimental import pallas as pl
from jax.experimental.pallas import tpu as pltpu
from jax.sharding import PartitionSpec as P

HEAD_DIM = 32
ROW_REACH = 1
COL_REACH = 2
GROUP = 128 // HEAD_DIM
EPSILON = 1e-06
SCALE = HEAD_DIM ** (-0.5)
SQRT_HALF = 0.5**0.5
PHI_SCALE = (2.0 * math.pi) ** (-0.5)
NEGATIVE = -1e30
CUT = 1024
PACE = 2
ORDERS = (("zxyw", "xyzw"), ("yzxw", "zywx"), ("yxzw", "xyzw"))
ORDER = (2, 3, 1, 3, 2, 1, 3, 2, 1, 3, 2, 1, 3, 2, 1, 2, 3, 1, 2, 3, 1, 3, 2, 1, 3, 2, 1, 3)

f32 = jnp.float32
bf16 = jnp.bfloat16
MIB = 1024 * 1024


def dot_nn(left, right):
    return lax.dot_general(left, right, (((1,), (0,)), ((), ())), preferred_element_type=f32)


def dot_nt(left, right):
    return lax.dot_general(left, right, (((1,), (1,)), ((), ())), preferred_element_type=f32)


def dot_tn(left, right):
    return lax.dot_general(left, right, (((0,), (0,)), ((), ())), preferred_element_type=f32)


def normed(values):
    mean = jnp.mean(values, axis=-1, keepdims=True)
    centred = values - mean
    spread = jnp.mean(centred * centred, axis=-1, keepdims=True)
    scale = lax.rsqrt(spread + EPSILON)
    return centred * scale, scale


def norm_back(grad, gain, unit, scale):
    scaled = grad * gain
    first = jnp.mean(scaled, axis=-1, keepdims=True)
    second = jnp.mean(scaled * unit, axis=-1, keepdims=True)
    return scale * (scaled - first - unit * second)


def as_row(ref):
    return ref[...].astype(f32).reshape(1, ref.shape[0])


def stack_heads(block, lane_head):
    zero = jnp.zeros_like(block)
    return jnp.concatenate(
        [jnp.where(lane_head == head, block, zero) for head in range(GROUP)], axis=0
    )


def fold_heads(stacked, lane_head, rows):
    total = jnp.where(lane_head == 0, stacked[:rows], 0.0)
    for head in range(1, GROUP):
        total = jnp.where(lane_head == head, stacked[head * rows : (head + 1) * rows], total)
    return total


def window_bias(axes, steps, lat_dev, lon):
    band = steps * lat_dev * lon
    keys = band + 2 * steps * lon
    query = lax.broadcasted_iota(jnp.int32, (band, keys), 0)
    key = lax.broadcasted_iota(jnp.int32, (band, keys), 1)
    query_row = query // lon % lat_dev
    first = jnp.where(axes.has_below(), -1, -2 - ROW_REACH)
    last = jnp.where(axes.has_above(), lat_dev, lat_dev + 1 + ROW_REACH)
    key_row = jnp.where(
        key < band, key // lon % lat_dev, jnp.where(key < band + steps * lon, first, last)
    )
    gap = jnp.abs(query % lon - key % lon)
    gap = jnp.minimum(gap, lon - gap)
    seen = (jnp.abs(query_row - key_row) <= ROW_REACH) & (gap <= COL_REACH)
    return jnp.where(seen, 0.0, NEGATIVE)


def block_kernel(
    axes,
    shards,
    items,
    steps,
    lat_dev,
    lon,
    *refs,
):
    sources, finals, refs = refs[:16], refs[16:29], refs[29:]
    targets, locals_, refs = refs[:16], refs[16:29], refs[29:]
    kv_ref, q_ref, p_ref, do_ref, o_ref, c_ref, g_ref, du_ref, dy_ref, in_sems, out_sems = refs
    fetches = start_copies(sources, targets, in_sems)
    (tok, gain1, bias1, qv_bias, beside, across, wqkv, wproj) = targets[:8]
    (bproj, gain2, bias2, w1, b1, w2, b2, cot) = targets[8:]
    (mixed_out, a_out, dx1_out, small_out, keep1, send1, keep2, send2) = locals_[:8]
    (dq_out, dk_out, dv_out, to_beside, to_across) = locals_[8:]
    leaving = []

    def leave(index, slot=0, window=None):
        source, target = locals_[index], finals[index]
        if window is not None:
            source, target = source.at[window], target.at[window]
        copy = pltpu.make_async_copy(source, target, out_sems.at[index, slot])
        copy.start()
        leaving.append(copy)

    for copy in fetches[:6]:
        copy.wait()
    rows, width = tok.shape
    hidden = w1.shape[1]
    side = beside.shape[0]
    band = rows // items
    edge = side // items
    groups = width // 128
    lane_head = lax.broadcasted_iota(jnp.int32, (1, 128), 1) // HEAD_DIM

    g1 = as_row(gain1)
    h1 = as_row(bias1)
    x = tok[...].astype(f32)
    unit, _ = normed(x)
    a_own = (unit * g1 + h1).astype(bf16)
    a_out[...] = a_own
    leave(1)
    wide = jnp.concatenate([beside[...], across[...]], axis=0).astype(f32)
    unit_wide, _ = normed(wide)
    a_wide = (unit_wide * g1 + h1).astype(bf16)
    a_all = jnp.concatenate([a_own, a_wide], axis=0)
    fetches[6].wait()
    q_ref[...] = (dot_nn(a_own, wqkv[:, :width]) + qv_bias[0:1, :].astype(f32)).astype(bf16)
    kv_ref[0] = dot_nn(a_all, wqkv[:, width : 2 * width]).astype(bf16)
    kv_ref[1] = (dot_nn(a_all, wqkv[:, 2 * width :]) + qv_bias[1:2, :].astype(f32)).astype(bf16)

    window = jnp.concatenate([window_bias(axes, steps, lat_dev, lon)] * GROUP, axis=0)
    odd = axes.bit(axes.core)
    below = pl.multiple_of(rows + (1 - odd) * side, 16)
    above = pl.multiple_of(rows + odd * side, 16)

    def keys_of(which, item, lanes):
        return jnp.concatenate(
            [
                kv_ref[which, item * band : (item + 1) * band, lanes],
                kv_ref[which, pl.ds(below + item * edge, edge), lanes],
                kv_ref[which, pl.ds(above + item * edge, edge), lanes],
            ],
            axis=0,
        )

    for item in range(items):
        for group in range(groups):
            lanes = slice(group * 128, (group + 1) * 128)
            own = slice(item * band, (item + 1) * band)
            queries = stack_heads(q_ref[own, lanes], lane_head)
            scores = dot_nt(queries, keys_of(0, item, lanes)) * SCALE + window
            top = jnp.max(scores, axis=-1, keepdims=True)
            weights = jnp.exp(scores - top)
            total = jnp.sum(weights, axis=-1, keepdims=True)
            soft = weights * (1.0 / total)
            p_ref[item * groups + group] = soft
            mixed_heads = dot_nn(soft.astype(bf16), keys_of(1, item, lanes))
            o_ref[own, lanes] = fold_heads(mixed_heads, lane_head, band).astype(bf16)

    for copy in fetches[7:]:
        copy.wait()
    g2 = as_row(gain2)
    h2 = as_row(bias2)
    x1 = x + dot_nn(o_ref[...], wproj[...]) + as_row(bproj)
    unit2, scale2 = normed(x1)
    c_low = (unit2 * g2 + h2).astype(bf16)
    c_ref[...] = c_low
    cot_low = cot[...]
    branch = jnp.zeros((rows, width), f32)
    dc = jnp.zeros((rows, width), f32)
    b1_row = as_row(b1)
    for part in range(hidden // width):
        cols = slice(part * width, (part + 1) * width)
        u = dot_nn(c_low, w1[:, cols]) + b1_row[:, cols]
        cdf = 0.5 + 0.5 * lax.erf(u * SQRT_HALF)
        slope = cdf + u * (jnp.exp(u * u * -0.5) * PHI_SCALE)
        act = (u * cdf).astype(bf16)
        g_ref[:, cols] = act
        branch = branch + dot_nn(act, w2[cols, :])
        dh = dot_nt(cot_low, w2[cols, :])
        du_low = (dh * slope).astype(bf16)
        du_ref[:, cols] = du_low
        small_out[4 + part : 5 + part, :] = jnp.sum(du_low.astype(f32), axis=0, keepdims=True)
        dc = dc + dot_nt(du_low, w1[:, cols])
    mixed_out[...] = (x1 + branch + as_row(b2)).astype(bf16)
    cot_wide = cot_low.astype(f32)
    small_out[0:1, :] = jnp.sum(dc * unit2, axis=0, keepdims=True)
    small_out[1:2, :] = jnp.sum(dc, axis=0, keepdims=True)
    small_out[2:3, :] = jnp.sum(cot_wide, axis=0, keepdims=True)
    dx1 = cot_wide + norm_back(dc, g2, unit2, scale2)
    dx1_out[...] = dx1
    leave(0)
    leave(2)
    dy = dx1.astype(bf16)
    dy_ref[...] = dy
    small_out[3:4, :] = jnp.sum(dy.astype(f32), axis=0, keepdims=True)
    do_ref[...] = dot_nt(dy, wproj[...]).astype(bf16)
    leave(3)
    jobs = grad_jobs(axes, 1, shards, c_ref, du_ref, keep2, send2)
    jobs += grad_jobs(axes, 1, shards, o_ref, dy_ref, keep2, send2, hidden)
    jobs.append(lambda: (leave(6), leave(7)))
    jobs += grad_jobs(axes, 0, shards, g_ref, cot, keep1, send1)
    jobs.append(lambda: (leave(4), leave(5)))

    for item in range(items):
        for group in range(groups):
            lanes = slice(group * 128, (group + 1) * 128)
            own = slice(item * band, (item + 1) * band)
            ends = slice(item * edge, (item + 1) * edge)
            for _ in range(PACE):
                if jobs:
                    jobs.pop(0)()
            grads = stack_heads(do_ref[own, lanes], lane_head)
            queries = stack_heads(q_ref[own, lanes], lane_head)
            soft = p_ref[item * groups + group]
            dp = dot_nt(grads, keys_of(1, item, lanes))
            inner = jnp.sum(soft * dp, axis=-1, keepdims=True)
            ds = (soft * (dp - inner)).astype(bf16)
            dq = fold_heads(dot_nn(ds, keys_of(0, item, lanes)), lane_head, band) * SCALE
            dq_out[own, lanes] = dq.astype(bf16)
            dk = dot_tn(ds, queries) * SCALE
            dv = dot_tn(soft.astype(bf16), grads)
            dk_out[own, lanes] = dk[:band]
            dv_out[own, lanes] = dv[:band]
            for index, grad in ((0, dk), (1, dv)):
                down = grad[band : band + edge]
                up = grad[band + edge :]
                to_beside[index, ends, lanes] = jnp.where(odd == 1, down, up).astype(bf16)
                to_across[index, ends, lanes] = jnp.where(odd == 1, up, down).astype(bf16)
        for index in (8, 9, 10):
            leave(index, item, (own, slice(None)))
        for index in (11, 12):
            leave(index, item, (slice(None), ends, slice(None)))
    for copy in leaving:
        copy.wait()


def start_copies(sources, targets, sems, first=0):
    copies = [
        pltpu.make_async_copy(source, target, sems.at[first + index])
        for index, (source, target) in enumerate(zip(sources, targets))
    ]
    for copy in copies:
        copy.start()
    return copies


def grad_jobs(axes, stream, shards, left, right, keep, send, first=0):
    half = left.shape[1] // 2
    per = half // shards
    step = min(half, 256)
    width = min(right.shape[1], CUT)
    core = axes.bit(axes.core)
    jobs = []
    for ref, owner in ((keep, core), (send, 1 - core)):
        slot = axes.slot(stream, owner)
        for start in range(0, half, step):
            for column in range(0, right.shape[1], width):

                def job(ref=ref, owner=owner, slot=slot, start=start, column=column):
                    columns = pl.ds(pl.multiple_of(owner * half + start, 128), step)
                    end = min(column + width, right.shape[1])
                    product = dot_tn(left[:, columns], right[:, column:end])
                    lanes = slice(first + column, first + end)
                    for index in range(step // per):
                        spot = pl.multiple_of(((start // per + index) ^ slot) * per, per)
                        rows = slice(index * per, (index + 1) * per)
                        ref[pl.ds(spot, per), lanes] = product[rows].astype(bf16)

                jobs.append(job)
    return jobs


def qkv_grad_kernel(
    axes,
    shards,
    lat_dev,
    lon,
    *refs,
):
    sources, finals, refs = refs[:11], refs[11:15], refs[15:]
    targets, locals_, refs = refs[:11], refs[11:15], refs[15:]
    joined, in_sems, out_sems = refs
    fetches = start_copies(sources, targets, in_sems)
    dq, dk, dv, from_beside, from_across, a_low, wqkv, tok, gain1, dx1, small_in = targets
    keep, send, tokens_out, small_out = locals_
    for copy in fetches[:6]:
        copy.wait()
    rows, width = tok.shape
    joined[:, :width] = dq[...]
    odd = axes.bit(axes.core) == 1
    for which, grads in ((0, dk), (1, dv)):
        columns = slice((1 + which) * width, (2 + which) * width)
        for strip in range(rows // (lat_dev * lon)):
            edge = slice(strip * lon, (strip + 1) * lon)
            for row in range(lat_dev):
                start = (strip * lat_dev + row) * lon
                value = grads[start : start + lon, :]
                near = from_beside[which, edge, :].astype(f32)
                far = from_across[which, edge, :].astype(f32)
                if row == 0:
                    value = value + jnp.where(odd, near, far)
                if row == lat_dev - 1:
                    value = value + jnp.where(odd, far, near)
                joined[start : start + lon, columns] = value.astype(bf16)
    for job in grad_jobs(axes, 2, shards, a_low, joined, keep, send):
        job()
    leaving = start_copies(locals_[:2], finals[:2], out_sems)
    for copy in fetches[6:]:
        copy.wait()
    da = dot_nt(joined[...], wqkv[...])
    unit, scale = normed(tok[...].astype(f32))
    grad = dx1[...] + norm_back(da, as_row(gain1), unit, scale)
    tokens_out[...] = grad.astype(bf16)
    sums = [
        jnp.sum(da * unit, axis=0, keepdims=True),
        jnp.sum(da, axis=0, keepdims=True),
        jnp.sum(joined[:, :width].astype(f32), axis=0, keepdims=True),
        jnp.sum(joined[:, 2 * width :].astype(f32), axis=0, keepdims=True),
    ] + [small_in[index : index + 1, :] for index in range(small_in.shape[0])]
    for index, row in enumerate(sums):
        place_of = slice(index % 3 * width, (index % 3 + 1) * width)
        small_out[index // 3 : index // 3 + 1, place_of] = row.astype(bf16)
    leaving += start_copies(locals_[2:], finals[2:], out_sems, 2)
    for copy in leaving:
        copy.wait()


def spread_kernel(axes, shards, streams, other, sums, *refs):
    count = sum(len(widths) for _, widths in streams)
    pieces = refs[: len(streams)]
    outs = refs[-2 * (count + len(sums)) - 1 : -count - len(sums) - 1]
    wide, sems = refs[-count - len(sums) - 1 : -1], refs[-1]
    core = axes.bit(axes.core)
    owner = 1 - core if other else core
    copies = []

    def leave(source, target, index, part):
        copy = pltpu.make_async_copy(source, target, sems.at[index, part])
        copy.start()
        copies.append(copy)

    number = 0
    for piece, (stream, widths) in zip(pieces, streams):
        slot = axes.slot(stream, owner)
        per = outs[number].shape[0] // (2 * shards)
        for index in range(shards):
            spot = pl.multiple_of((owner * shards + (index ^ slot)) * per, per)
            rows = slice(index * per, (index + 1) * per)
            first = 0
            for part, width in enumerate(widths, number):
                wide[part][rows, :] = piece[rows, first : first + width].astype(f32)
                first += width
                leave(wide[part].at[rows, :], outs[part].at[pl.ds(spot, per), :], index, part)
        number += len(widths)
    if sums:
        rows = slice(shards * per, pieces[-1].shape[0])
        total = refs[len(streams)][rows, :].astype(f32) + pieces[-1][rows, :].astype(f32)
        width = total.shape[1] // 3
        taken = [
            total[k // 3 : k // 3 + 1, k % 3 * width : (k % 3 + 1) * width]
            for k in range(3 * total.shape[0])
        ]
        for part, (first, shape) in enumerate(sums):
            buffer = wide[count + part]
            for k in range(math.prod(shape) // width):
                if len(shape) == 1:
                    buffer[k * width : (k + 1) * width] = taken[first + k].reshape(width)
                else:
                    buffer[k : k + 1, :] = taken[first + k]
            leave(buffer, outs[count + part], part, count)
    for copy in copies:
        copy.wait()


def spread(axes, shards, streams, rows, pieces, outs=(), sums=()):
    hbm = pl.BlockSpec(memory_space=pltpu.HBM)
    shapes = [(count, width) for (_, widths), count in zip(streams, rows) for width in widths]
    halves = [(count // 2, width) for count, width in shapes]
    shapes += [shape for _, shape in sums]
    return pl.pallas_call(
        functools.partial(spread_kernel, axes, shards, streams, bool(outs), sums),
        out_shape=[jax.ShapeDtypeStruct(shape, f32) for shape in shapes],
        in_specs=[pl.BlockSpec(memory_space=pltpu.VMEM)] * len(pieces) + [hbm] * len(outs),
        out_specs=[hbm] * len(shapes),
        scratch_shapes=[pltpu.VMEM(shape, f32) for shape in halves]
        + [pltpu.VMEM(shape, f32) for _, shape in sums]
        + [pltpu.SemaphoreType.DMA((max(shards, len(sums)), len(halves) + 1))],
        input_output_aliases={len(pieces) + index: index for index in range(len(outs))},
        compiler_params=pltpu.CompilerParams(vmem_limit_bytes=(4 + 4 * len(streams)) * MIB),
        cost_estimate=pl.CostEstimate(
            flops=0,
            bytes_accessed=6 * sum(math.prod(shape) for shape in halves),
            transcendentals=0,
        ),
    )(*pieces, *outs)


def on_device(kernel, operands, outs, scratch=(), sems=(), flops=0):
    buffers = [pltpu.VMEM(value.shape, value.dtype) for value in operands]
    buffers += [pltpu.VMEM(shape, jnp.dtype(dtype)) for shape, dtype in outs]
    hbm = pl.BlockSpec(memory_space=pltpu.HBM)
    return pl.pallas_call(
        kernel,
        out_shape=[jax.ShapeDtypeStruct(shape, dtype) for shape, dtype in outs],
        in_specs=[hbm] * len(operands),
        out_specs=[hbm] * len(outs),
        scratch_shapes=buffers
        + [pltpu.VMEM(shape, dtype) for shape, dtype in scratch]
        + [pltpu.SemaphoreType.DMA(shape) for shape in sems],
        compiler_params=pltpu.CompilerParams(vmem_limit_bytes=60 * MIB),
        cost_estimate=pl.CostEstimate(
            flops=flops,
            bytes_accessed=sum(math.prod(buffer.shape) * buffer.dtype.itemsize for buffer in buffers),
            transcendentals=0,
        ),
    )(*operands)


class Axes:
    def __init__(self, mesh):
        self.sizes = dict(mesh.shape)
        bits = self.sizes["items"].bit_length() - 1
        self.core = ("lat", 1)
        named = {"x": ("lat", 2), "y": ("items", 1), "z": ("items", 2), "w": ("items", 4)}
        self.orders = [[[named[key] for key in order] for order in pair] for pair in ORDERS]
        self.extra = [("items", 1 << bit) for bit in range(3, bits)]

    def bit(self, dim):
        axis, value = dim
        return (lax.axis_index(axis) // value) % 2

    def slot(self, stream, core):
        pair = []
        for order in self.orders[stream]:
            total = 0
            for dim in order[:-1]:
                total = total * 2 + self.bit(dim)
            pair.append(total)
        return jnp.where(core == 0, pair[0], pair[1])

    def has_below(self):
        return lax.axis_index("lat") > 0

    def has_above(self):
        return lax.axis_index("lat") < self.sizes["lat"] - 1

    def beside(self, value):
        return self.exchange(value, (self.core, self.core))

    def across(self, value):
        count = self.sizes["lat"]
        pairs = [(index, (index + 1) // 2 * 4 - 1 - index) for index in range(1, count - 1)]
        return lax.ppermute(value, "lat", pairs)

    def exchange(self, value, dims):
        items = self.sizes["items"]
        pairs = []
        for index in range(self.sizes["lat"] * items):
            axis, bit = dims[index // items % 2]
            pairs.append((index, index ^ (bit * items if axis == "lat" else bit)))
        return lax.ppermute(value, ("lat", "items"), pairs)


def add_rows(terms, low, high):
    total = terms[0][low:high].astype(f32)
    for term in terms[1:]:
        total = total + term[low:high].astype(f32)
    return total


def after(value, token):
    return lax.optimization_barrier((value, token))[0]


class Sequence:
    def __init__(self, axes, token):
        self.axes = axes
        self.token = token

    def ready(self, value):
        return after(value, self.token)

    def swap(self, value, dims, scope="swap"):
        self.token = value
        with jax.named_scope(scope):
            return self.axes.exchange(value, dims)


def sum_stream(sequence, stream, keep, send, write, small=None):
    axes = sequence.axes
    core = (axes.core, axes.core)
    label = (f"s{stream + 1}h{hop}" for hop in range(99))
    got = sequence.swap(send, core, next(label))
    yield
    terms = [keep, sequence.ready(got)]
    rows = keep.shape[0]
    extra = 0 if small is None else small.shape[0]
    pairs = list(zip(*axes.orders[stream]))
    hops, whole = pairs[:-1], pairs[-1:] + [(dim, dim) for dim in axes.extra]
    for dims in hops:
        rows //= 2
        value = add_rows(terms, rows, 2 * rows).astype(bf16)
        if extra:
            value = jnp.concatenate([value, small], axis=0)
        got = sequence.swap(value, dims, next(label))
        yield
        got = sequence.ready(got)
        if extra:
            small = (small.astype(f32) + got[rows:].astype(f32)).astype(bf16)
        terms.append(got)
    piece = add_rows(terms, 0, rows).astype(bf16)
    for dims in whole:
        value = jnp.concatenate([piece, small], axis=0) if extra else piece
        got = sequence.swap(value, dims, next(label))
        yield
        got = sequence.ready(got)
        if extra:
            small = (small.astype(f32) + got[rows:].astype(f32)).astype(bf16)
        piece = (piece.astype(f32) + got[:rows].astype(f32)).astype(bf16)
    for dims in reversed(hops):
        got = sequence.swap(piece, dims, next(label))
        yield
        parts = [piece, sequence.ready(got)]
        if extra and dims is hops[0]:
            parts.append(small)
        piece = jnp.concatenate(parts, axis=0)
    near = sequence.swap(piece, core, next(label))
    write(piece)
    yield
    write(piece, near)


def body(
    axes,
    tokens,
    norm1_gain,
    norm1_bias,
    qkv_weight,
    qv_bias,
    proj_weight,
    proj_bias,
    norm2_gain,
    norm2_bias,
    fc1_weight,
    fc1_bias,
    fc2_weight,
    fc2_bias,
    cotangent,
):
    items, steps, lat_dev, lon, width = tokens.shape
    hidden = fc1_weight.shape[1]
    rows = items * steps * lat_dev * lon
    side = items * steps * lon
    lat_total = axes.sizes["lat"]
    shards = 8
    odd = axes.bit(axes.core) == 1
    first = tokens[:, :, 0].reshape(side, width)
    last = tokens[:, :, lat_dev - 1].reshape(side, width)
    beside = axes.beside(jnp.where(odd, first, last))
    across = axes.across(jnp.where(odd, last, first))
    flat_tokens = tokens.reshape(rows, width)
    flat_cot = cotangent.reshape(rows, width)
    operands = (
        flat_tokens,
        norm1_gain,
        norm1_bias,
        qv_bias,
        beside,
        across,
        qkv_weight,
        proj_weight,
        proj_bias,
        norm2_gain,
        norm2_bias,
        fc1_weight,
        fc1_bias,
        fc2_weight,
        fc2_bias,
        flat_cot,
    )
    band = rows // items
    keys = band + 2 * side // items
    groups = width // 128
    both = hidden + width
    (mixed, a_low, dx1, small, keep1, send1, keep2, send2, dq, dk, dv, to_beside, to_across) = on_device(
        functools.partial(block_kernel, axes, shards, items, steps, lat_dev, lon),
        operands,
        [
            ((rows, width), bf16),
            ((rows, width), bf16),
            ((rows, width), f32),
            ((4 + hidden // width, width), f32),
            ((hidden // 2, width), bf16),
            ((hidden // 2, width), bf16),
            ((width // 2, both), bf16),
            ((width // 2, both), bf16),
            ((rows, width), bf16),
            ((rows, width), f32),
            ((rows, width), f32),
            ((2, side, width), bf16),
            ((2, side, width), bf16),
        ],
        scratch=[
            ((2, rows + 2 * side, width), bf16),
            ((rows, width), bf16),
            ((items * groups, GROUP * band, keys), f32),
            ((rows, width), bf16),
            ((rows, width), bf16),
            ((rows, width), bf16),
            ((rows, hidden), bf16),
            ((rows, hidden), bf16),
            ((rows, width), bf16),
        ],
        sems=[(16,), (13, items)],
        flops=2 * rows * width * (4 * width + 6 * hidden),
    )

    from_beside = axes.beside(to_beside)
    from_across = axes.across(to_across)
    sequence = Sequence(axes, (to_beside, to_across))
    grads = {}
    splits = {1: (width,), 2: (hidden, width), 3: (3 * width,)}

    last = {}
    rows_of = {1: hidden, 2: width, 3: width}

    def stream(name, keep, send, small=None):
        def write(own, other=None):
            if other is None:
                grads[name] = spread(axes, shards, ((name - 1, splits[name]),), (rows_of[name],), (own,))
                sequence.token = grads[name][0]
            last[name] = own, other

        return sum_stream(sequence, name - 1, keep, send, write, small)

    small_places = (
        (0, (width,)),
        (1, (width,)),
        (2, (2, width)),
        (7, (width,)),
        (4, (width,)),
        (5, (width,)),
        (8, (hidden,)),
        (6, (width,)),
    )
    streams = {1: stream(1, keep1, send1), 2: stream(2, keep2, send2)}
    next(streams[2])
    next(streams[1])
    sequence.token = from_beside

    def join():
        operands = (
            after(dq, sequence.token),
            dk,
            dv,
            from_beside,
            from_across,
            a_low,
            qkv_weight,
            flat_tokens,
            norm1_gain,
            dx1,
            small,
        )
        keep, send, grad, sums = on_device(
            functools.partial(qkv_grad_kernel, axes, shards, lat_dev, lon),
            operands,
            [
                ((width // 2, 3 * width), bf16),
                ((width // 2, 3 * width), bf16),
                ((rows, width), bf16),
                (((8 + hidden // width) // 3, 3 * width), bf16),
            ],
            scratch=[((rows, 3 * width), bf16)],
            sems=[(11,), (4,)],
            flops=12 * rows * width * width,
        )
        streams[3] = stream(3, keep, send, sums)
        return grad

    for name in ORDER + (1, 2, 3) * 12:
        if name not in streams:
            tokens_grad = join()
        next(streams[name], None)
    grad_fc2, grad_fc1, grad_proj, grad_qkv, *sums = spread(
        axes,
        shards,
        tuple((name - 1, splits[name]) for name in (1, 2, 3)),
        tuple(rows_of[name] for name in (1, 2, 3)),
        tuple(last[name][1] for name in (1, 2, 3)) + (last[3][0],),
        tuple(out for name in (1, 2, 3) for out in grads[name]),
        small_places,
    )
    return (
        mixed.reshape(tokens.shape),
        tokens_grad.reshape(tokens.shape),
        sums[0],
        sums[1],
        grad_qkv,
        sums[2],
        grad_proj,
        sums[3],
        sums[4],
        sums[5],
        grad_fc1,
        sums[6],
        grad_fc2,
        sums[7],
    )


def solution(mesh):
    split = P("items", None, "lat", None, None)
    whole = P()
    return jax.shard_map(
        functools.partial(body, Axes(mesh)),
        mesh=mesh,
        in_specs=(split,) + (whole,) * 12 + (split,),
        out_specs=(split, split) + (whole,) * 12,
        check_vma=False,
    )
```

```python
import functools
import math

import jax
import jax.numpy as jnp
from jax import lax
from jax.experimental import pallas as pl
from jax.experimental.pallas import tpu as pltpu
from jax.sharding import PartitionSpec as P

HEAD_DIM = 32
ROW_REACH = 1
COL_REACH = 2
GROUP = 128 // HEAD_DIM
EPSILON = 1e-06
SCALE = HEAD_DIM ** (-0.5)
SQRT_HALF = 0.5**0.5
PHI_SCALE = (2.0 * math.pi) ** (-0.5)
NEGATIVE = -1e30
CUT = 1024
PACE = 2
ORDERS = (("zxyw", "xyzw"), ("yzxw", "zywx"), ("yxzw", "xyzw"))
ORDER = (2, 3, 1, 3, 2, 1, 3, 2, 1, 3, 2, 1, 3, 2, 1, 2, 3, 1, 2, 3, 1, 3, 2, 1, 3, 2, 1, 3)

f32 = jnp.float32
bf16 = jnp.bfloat16
MIB = 1024 * 1024


def dot_nn(left, right):
    return lax.dot_general(left, right, (((1,), (0,)), ((), ())), preferred_element_type=f32)


def dot_nt(left, right):
    return lax.dot_general(left, right, (((1,), (1,)), ((), ())), preferred_element_type=f32)


def dot_tn(left, right):
    return lax.dot_general(left, right, (((0,), (0,)), ((), ())), preferred_element_type=f32)


def normed(values):
    mean = jnp.mean(values, axis=-1, keepdims=True)
    centred = values - mean
    spread = jnp.mean(centred * centred, axis=-1, keepdims=True)
    scale = lax.rsqrt(spread + EPSILON)
    return centred * scale, scale


def norm_back(grad, gain, unit, scale):
    scaled = grad * gain
    first = jnp.mean(scaled, axis=-1, keepdims=True)
    second = jnp.mean(scaled * unit, axis=-1, keepdims=True)
    return scale * (scaled - first - unit * second)


def as_row(ref):
    return ref[...].astype(f32).reshape(1, ref.shape[0])


def stack_heads(block, lane_head):
    zero = jnp.zeros_like(block)
    return jnp.concatenate(
        [jnp.where(lane_head == head, block, zero) for head in range(GROUP)], axis=0
    )


def fold_heads(stacked, lane_head, rows):
    total = jnp.where(lane_head == 0, stacked[:rows], 0.0)
    for head in range(1, GROUP):
        total = jnp.where(lane_head == head, stacked[head * rows : (head + 1) * rows], total)
    return total


def window_bias(axes, steps, lat_dev, lon):
    band = steps * lat_dev * lon
    keys = band + 2 * steps * lon
    query = lax.broadcasted_iota(jnp.int32, (band, keys), 0)
    key = lax.broadcasted_iota(jnp.int32, (band, keys), 1)
    query_row = query // lon % lat_dev
    first = jnp.where(axes.has_below(), -1, -2 - ROW_REACH)
    last = jnp.where(axes.has_above(), lat_dev, lat_dev + 1 + ROW_REACH)
    key_row = jnp.where(
        key < band, key // lon % lat_dev, jnp.where(key < band + steps * lon, first, last)
    )
    gap = jnp.abs(query % lon - key % lon)
    gap = jnp.minimum(gap, lon - gap)
    seen = (jnp.abs(query_row - key_row) <= ROW_REACH) & (gap <= COL_REACH)
    return jnp.where(seen, 0.0, NEGATIVE)


def block_kernel(
    axes,
    shards,
    items,
    steps,
    lat_dev,
    lon,
    *refs,
):
    sources, finals, refs = refs[:16], refs[16:29], refs[29:]
    targets, locals_, refs = refs[:16], refs[16:29], refs[29:]
    kv_ref, q_ref, p_ref, do_ref, o_ref, c_ref, g_ref, du_ref, dy_ref, in_sems, out_sems = refs
    fetches = start_copies(sources, targets, in_sems)
    (tok, gain1, bias1, qv_bias, beside, across, wqkv, wproj) = targets[:8]
    (bproj, gain2, bias2, w1, b1, w2, b2, cot) = targets[8:]
    (mixed_out, a_out, dx1_out, small_out, keep1, send1, keep2, send2) = locals_[:8]
    (dq_out, dk_out, dv_out, to_beside, to_across) = locals_[8:]
    leaving = []

    def leave(index, slot=0, window=None):
        source, target = locals_[index], finals[index]
        if window is not None:
            source, target = source.at[window], target.at[window]
        copy = pltpu.make_async_copy(source, target, out_sems.at[index, slot])
        copy.start()
        leaving.append(copy)

    for copy in fetches[:6]:
        copy.wait()
    rows, width = tok.shape
    hidden = w1.shape[1]
    side = beside.shape[0]
    band = rows // items
    edge = side // items
    groups = width // 128
    lane_head = lax.broadcasted_iota(jnp.int32, (1, 128), 1) // HEAD_DIM

    g1 = as_row(gain1)
    h1 = as_row(bias1)
    x = tok[...].astype(f32)
    unit, _ = normed(x)
    a_own = (unit * g1 + h1).astype(bf16)
    a_out[...] = a_own
    leave(1)
    wide = jnp.concatenate([beside[...], across[...]], axis=0).astype(f32)
    unit_wide, _ = normed(wide)
    a_wide = (unit_wide * g1 + h1).astype(bf16)
    a_all = jnp.concatenate([a_own, a_wide], axis=0)
    fetches[6].wait()
    q_ref[...] = (dot_nn(a_own, wqkv[:, :width]) + qv_bias[0:1, :].astype(f32)).astype(bf16)
    kv_ref[0] = dot_nn(a_all, wqkv[:, width : 2 * width]).astype(bf16)
    kv_ref[1] = (dot_nn(a_all, wqkv[:, 2 * width :]) + qv_bias[1:2, :].astype(f32)).astype(bf16)

    window = jnp.concatenate([window_bias(axes, steps, lat_dev, lon)] * GROUP, axis=0)
    odd = axes.bit(axes.core)
    below = pl.multiple_of(rows + (1 - odd) * side, 16)
    above = pl.multiple_of(rows + odd * side, 16)

    def keys_of(which, item, lanes):
        return jnp.concatenate(
            [
                kv_ref[which, item * band : (item + 1) * band, lanes],
                kv_ref[which, pl.ds(below + item * edge, edge), lanes],
                kv_ref[which, pl.ds(above + item * edge, edge), lanes],
            ],
            axis=0,
        )

    for item in range(items):
        for group in range(groups):
            lanes = slice(group * 128, (group + 1) * 128)
            own = slice(item * band, (item + 1) * band)
            queries = stack_heads(q_ref[own, lanes], lane_head)
            scores = dot_nt(queries, keys_of(0, item, lanes)) * SCALE + window
            top = jnp.max(scores, axis=-1, keepdims=True)
            weights = jnp.exp(scores - top)
            total = jnp.sum(weights, axis=-1, keepdims=True)
            soft = weights * (1.0 / total)
            p_ref[item * groups + group] = soft
            mixed_heads = dot_nn(soft.astype(bf16), keys_of(1, item, lanes))
            o_ref[own, lanes] = fold_heads(mixed_heads, lane_head, band).astype(bf16)

    for copy in fetches[7:]:
        copy.wait()
    g2 = as_row(gain2)
    h2 = as_row(bias2)
    x1 = x + dot_nn(o_ref[...], wproj[...]) + as_row(bproj)
    unit2, scale2 = normed(x1)
    c_low = (unit2 * g2 + h2).astype(bf16)
    c_ref[...] = c_low
    cot_low = cot[...]
    branch = jnp.zeros((rows, width), f32)
    dc = jnp.zeros((rows, width), f32)
    b1_row = as_row(b1)
    for start in range(0, hidden, 1024):
        cols = slice(start, start + 1024)
        u = dot_nn(c_low, w1[:, cols]) + b1_row[:, cols]
        cdf = 0.5 + 0.5 * lax.erf(u * SQRT_HALF)
        slope = cdf + u * (jnp.exp(u * u * -0.5) * PHI_SCALE)
        act = (u * cdf).astype(bf16)
        g_ref[:, cols] = act
        branch = branch + dot_nn(act, w2[cols, :])
        dh = dot_nt(cot_low, w2[cols, :])
        du_low = (dh * slope).astype(bf16)
        du_ref[:, cols] = du_low
        sums = jnp.sum(du_low.astype(f32), axis=0, keepdims=True)
        for row in range(sums.shape[1] // width):
            place = 4 + start // width + row
            small_out[place : place + 1, :] = sums[:, row * width : (row + 1) * width]
        dc = dc + dot_nt(du_low, w1[:, cols])
    mixed_out[...] = (x1 + branch + as_row(b2)).astype(bf16)
    cot_wide = cot_low.astype(f32)
    small_out[0:1, :] = jnp.sum(dc * unit2, axis=0, keepdims=True)
    small_out[1:2, :] = jnp.sum(dc, axis=0, keepdims=True)
    small_out[2:3, :] = jnp.sum(cot_wide, axis=0, keepdims=True)
    dx1 = cot_wide + norm_back(dc, g2, unit2, scale2)
    dx1_out[...] = dx1
    leave(0)
    leave(2)
    dy = dx1.astype(bf16)
    dy_ref[...] = dy
    small_out[3:4, :] = jnp.sum(dy.astype(f32), axis=0, keepdims=True)
    do_ref[...] = dot_nt(dy, wproj[...]).astype(bf16)
    leave(3)
    jobs = grad_jobs(axes, 1, shards, c_ref, du_ref, keep2, send2)
    jobs += grad_jobs(axes, 1, shards, o_ref, dy_ref, keep2, send2, hidden)
    jobs.append(lambda: (leave(6), leave(7)))
    jobs += grad_jobs(axes, 0, shards, g_ref, cot, keep1, send1)
    jobs.append(lambda: (leave(4), leave(5)))

    for item in range(items):
        for group in range(groups):
            lanes = slice(group * 128, (group + 1) * 128)
            own = slice(item * band, (item + 1) * band)
            ends = slice(item * edge, (item + 1) * edge)
            for _ in range(PACE):
                if jobs:
                    jobs.pop(0)()
            grads = stack_heads(do_ref[own, lanes], lane_head)
            queries = stack_heads(q_ref[own, lanes], lane_head)
            soft = p_ref[item * groups + group]
            dp = dot_nt(grads, keys_of(1, item, lanes))
            inner = jnp.sum(soft * dp, axis=-1, keepdims=True)
            ds = (soft * (dp - inner)).astype(bf16)
            dq = fold_heads(dot_nn(ds, keys_of(0, item, lanes)), lane_head, band) * SCALE
            dq_out[own, lanes] = dq.astype(bf16)
            dk = dot_tn(ds, queries) * SCALE
            dv = dot_tn(soft.astype(bf16), grads)
            dk_out[own, lanes] = dk[:band]
            dv_out[own, lanes] = dv[:band]
            for index, grad in ((0, dk), (1, dv)):
                down = grad[band : band + edge]
                up = grad[band + edge :]
                to_beside[index, ends, lanes] = jnp.where(odd == 1, down, up).astype(bf16)
                to_across[index, ends, lanes] = jnp.where(odd == 1, up, down).astype(bf16)
        for index in (8, 9, 10):
            leave(index, item, (own, slice(None)))
        for index in (11, 12):
            leave(index, item, (slice(None), ends, slice(None)))
    for copy in leaving:
        copy.wait()


def start_copies(sources, targets, sems, first=0):
    copies = [
        pltpu.make_async_copy(source, target, sems.at[first + index])
        for index, (source, target) in enumerate(zip(sources, targets))
    ]
    for copy in copies:
        copy.start()
    return copies


def grad_jobs(axes, stream, shards, left, right, keep, send, first=0):
    half = left.shape[1] // 2
    per = half // shards
    step = min(half, 256)
    width = min(right.shape[1], CUT)
    core = axes.bit(axes.core)
    jobs = []
    for ref, owner in ((keep, core), (send, 1 - core)):
        slot = axes.slot(stream, owner)
        for start in range(0, half, step):
            for column in range(0, right.shape[1], width):

                def job(ref=ref, owner=owner, slot=slot, start=start, column=column):
                    columns = pl.ds(pl.multiple_of(owner * half + start, 128), step)
                    end = min(column + width, right.shape[1])
                    product = dot_tn(left[:, columns], right[:, column:end])
                    lanes = slice(first + column, first + end)
                    for index in range(step // per):
                        spot = pl.multiple_of(((start // per + index) ^ slot) * per, per)
                        rows = slice(index * per, (index + 1) * per)
                        ref[pl.ds(spot, per), lanes] = product[rows].astype(bf16)

                jobs.append(job)
    return jobs


def qkv_grad_kernel(
    axes,
    shards,
    lat_dev,
    lon,
    *refs,
):
    sources, finals, refs = refs[:11], refs[11:15], refs[15:]
    targets, locals_, refs = refs[:11], refs[11:15], refs[15:]
    joined, in_sems, out_sems = refs
    fetches = start_copies(sources, targets, in_sems)
    dq, dk, dv, from_beside, from_across, a_low, wqkv, tok, gain1, dx1, small_in = targets
    keep, send, tokens_out, small_out = locals_
    for copy in fetches[:6]:
        copy.wait()
    rows, width = tok.shape
    joined[:, :width] = dq[...]
    odd = axes.bit(axes.core) == 1
    for which, grads in ((0, dk), (1, dv)):
        columns = slice((1 + which) * width, (2 + which) * width)
        for strip in range(rows // (lat_dev * lon)):
            edge = slice(strip * lon, (strip + 1) * lon)
            for row in range(lat_dev):
                start = (strip * lat_dev + row) * lon
                value = grads[start : start + lon, :]
                near = from_beside[which, edge, :].astype(f32)
                far = from_across[which, edge, :].astype(f32)
                if row == 0:
                    value = value + jnp.where(odd, near, far)
                if row == lat_dev - 1:
                    value = value + jnp.where(odd, far, near)
                joined[start : start + lon, columns] = value.astype(bf16)
    for job in grad_jobs(axes, 2, shards, a_low, joined, keep, send):
        job()
    leaving = start_copies(locals_[:2], finals[:2], out_sems)
    for copy in fetches[6:]:
        copy.wait()
    da = dot_nt(joined[...], wqkv[...])
    unit, scale = normed(tok[...].astype(f32))
    grad = dx1[...] + norm_back(da, as_row(gain1), unit, scale)
    tokens_out[...] = grad.astype(bf16)
    sums = [
        jnp.sum(da * unit, axis=0, keepdims=True),
        jnp.sum(da, axis=0, keepdims=True),
        jnp.sum(joined[:, :width].astype(f32), axis=0, keepdims=True),
        jnp.sum(joined[:, 2 * width :].astype(f32), axis=0, keepdims=True),
    ] + [small_in[index : index + 1, :] for index in range(small_in.shape[0])]
    for index, row in enumerate(sums):
        place_of = slice(index % 3 * width, (index % 3 + 1) * width)
        small_out[index // 3 : index // 3 + 1, place_of] = row.astype(bf16)
    leaving += start_copies(locals_[2:], finals[2:], out_sems, 2)
    for copy in leaving:
        copy.wait()


def spread_kernel(axes, shards, streams, other, sums, *refs):
    count = sum(len(widths) for _, widths in streams)
    pieces = refs[: len(streams)]
    outs = refs[-2 * (count + len(sums)) - 1 : -count - len(sums) - 1]
    wide, sems = refs[-count - len(sums) - 1 : -1], refs[-1]
    core = axes.bit(axes.core)
    owner = 1 - core if other else core
    copies = []

    def leave(source, target, index, part):
        copy = pltpu.make_async_copy(source, target, sems.at[index, part])
        copy.start()
        copies.append(copy)

    number = 0
    for piece, (stream, widths) in zip(pieces, streams):
        slot = axes.slot(stream, owner)
        per = outs[number].shape[0] // (2 * shards)
        for index in range(shards):
            spot = pl.multiple_of((owner * shards + (index ^ slot)) * per, per)
            rows = slice(index * per, (index + 1) * per)
            first = 0
            for part, width in enumerate(widths, number):
                wide[part][rows, :] = piece[rows, first : first + width].astype(f32)
                first += width
                leave(wide[part].at[rows, :], outs[part].at[pl.ds(spot, per), :], index, part)
        number += len(widths)
    if sums:
        rows = slice(shards * per, pieces[-1].shape[0])
        total = refs[len(streams)][rows, :].astype(f32) + pieces[-1][rows, :].astype(f32)
        width = total.shape[1] // 3
        taken = [
            total[k // 3 : k // 3 + 1, k % 3 * width : (k % 3 + 1) * width]
            for k in range(3 * total.shape[0])
        ]
        for part, (first, shape) in enumerate(sums):
            buffer = wide[count + part]
            for k in range(math.prod(shape) // width):
                if len(shape) == 1:
                    buffer[k * width : (k + 1) * width] = taken[first + k].reshape(width)
                else:
                    buffer[k : k + 1, :] = taken[first + k]
            leave(buffer, outs[count + part], part, count)
    for copy in copies:
        copy.wait()


def spread(axes, shards, streams, rows, pieces, outs=(), sums=()):
    hbm = pl.BlockSpec(memory_space=pltpu.HBM)
    shapes = [(count, width) for (_, widths), count in zip(streams, rows) for width in widths]
    halves = [(count // 2, width) for count, width in shapes]
    shapes += [shape for _, shape in sums]
    return pl.pallas_call(
        functools.partial(spread_kernel, axes, shards, streams, bool(outs), sums),
        out_shape=[jax.ShapeDtypeStruct(shape, f32) for shape in shapes],
        in_specs=[pl.BlockSpec(memory_space=pltpu.VMEM)] * len(pieces) + [hbm] * len(outs),
        out_specs=[hbm] * len(shapes),
        scratch_shapes=[pltpu.VMEM(shape, f32) for shape in halves]
        + [pltpu.VMEM(shape, f32) for _, shape in sums]
        + [pltpu.SemaphoreType.DMA((max(shards, len(sums)), len(halves) + 1))],
        input_output_aliases={len(pieces) + index: index for index in range(len(outs))},
        compiler_params=pltpu.CompilerParams(vmem_limit_bytes=(4 + 4 * len(streams)) * MIB),
        cost_estimate=pl.CostEstimate(
            flops=0,
            bytes_accessed=6 * sum(math.prod(shape) for shape in halves),
            transcendentals=0,
        ),
    )(*pieces, *outs)


def on_device(kernel, operands, outs, scratch=(), sems=(), flops=0):
    buffers = [pltpu.VMEM(value.shape, value.dtype) for value in operands]
    buffers += [pltpu.VMEM(shape, jnp.dtype(dtype)) for shape, dtype in outs]
    hbm = pl.BlockSpec(memory_space=pltpu.HBM)
    return pl.pallas_call(
        kernel,
        out_shape=[jax.ShapeDtypeStruct(shape, dtype) for shape, dtype in outs],
        in_specs=[hbm] * len(operands),
        out_specs=[hbm] * len(outs),
        scratch_shapes=buffers
        + [pltpu.VMEM(shape, dtype) for shape, dtype in scratch]
        + [pltpu.SemaphoreType.DMA(shape) for shape in sems],
        compiler_params=pltpu.CompilerParams(vmem_limit_bytes=60 * MIB),
        cost_estimate=pl.CostEstimate(
            flops=flops,
            bytes_accessed=sum(math.prod(buffer.shape) * buffer.dtype.itemsize for buffer in buffers),
            transcendentals=0,
        ),
    )(*operands)


class Axes:
    def __init__(self, mesh):
        self.sizes = dict(mesh.shape)
        bits = self.sizes["items"].bit_length() - 1
        self.core = ("lat", 1)
        named = {"x": ("lat", 2), "y": ("items", 1), "z": ("items", 2), "w": ("items", 4)}
        self.orders = [[[named[key] for key in order] for order in pair] for pair in ORDERS]
        self.extra = [("items", 1 << bit) for bit in range(3, bits)]

    def bit(self, dim):
        axis, value = dim
        return (lax.axis_index(axis) // value) % 2

    def slot(self, stream, core):
        pair = []
        for order in self.orders[stream]:
            total = 0
            for dim in order[:-1]:
                total = total * 2 + self.bit(dim)
            pair.append(total)
        return jnp.where(core == 0, pair[0], pair[1])

    def has_below(self):
        return lax.axis_index("lat") > 0

    def has_above(self):
        return lax.axis_index("lat") < self.sizes["lat"] - 1

    def beside(self, value):
        return self.exchange(value, (self.core, self.core))

    def across(self, value):
        count = self.sizes["lat"]
        pairs = [(index, (index + 1) // 2 * 4 - 1 - index) for index in range(1, count - 1)]
        return lax.ppermute(value, "lat", pairs)

    def exchange(self, value, dims):
        items = self.sizes["items"]
        pairs = []
        for index in range(self.sizes["lat"] * items):
            axis, bit = dims[index // items % 2]
            pairs.append((index, index ^ (bit * items if axis == "lat" else bit)))
        return lax.ppermute(value, ("lat", "items"), pairs)


def add_rows(terms, low, high):
    total = terms[0][low:high].astype(f32)
    for term in terms[1:]:
        total = total + term[low:high].astype(f32)
    return total


def after(value, token):
    return lax.optimization_barrier((value, token))[0]


class Sequence:
    def __init__(self, axes, token):
        self.axes = axes
        self.token = token

    def ready(self, value):
        return after(value, self.token)

    def swap(self, value, dims, scope="swap"):
        self.token = value
        with jax.named_scope(scope):
            return self.axes.exchange(value, dims)


def sum_stream(sequence, stream, keep, send, write, small=None):
    axes = sequence.axes
    core = (axes.core, axes.core)
    label = (f"s{stream + 1}h{hop}" for hop in range(99))
    got = sequence.swap(send, core, next(label))
    yield
    terms = [keep, sequence.ready(got)]
    rows = keep.shape[0]
    extra = 0 if small is None else small.shape[0]
    pairs = list(zip(*axes.orders[stream]))
    hops, whole = pairs[:-1], pairs[-1:] + [(dim, dim) for dim in axes.extra]
    for dims in hops:
        rows //= 2
        value = add_rows(terms, rows, 2 * rows).astype(bf16)
        if extra:
            value = jnp.concatenate([value, small], axis=0)
        got = sequence.swap(value, dims, next(label))
        yield
        got = sequence.ready(got)
        if extra:
            small = (small.astype(f32) + got[rows:].astype(f32)).astype(bf16)
        terms.append(got)
    piece = add_rows(terms, 0, rows).astype(bf16)
    for dims in whole:
        value = jnp.concatenate([piece, small], axis=0) if extra else piece
        got = sequence.swap(value, dims, next(label))
        yield
        got = sequence.ready(got)
        if extra:
            small = (small.astype(f32) + got[rows:].astype(f32)).astype(bf16)
        piece = (piece.astype(f32) + got[:rows].astype(f32)).astype(bf16)
    for dims in reversed(hops):
        got = sequence.swap(piece, dims, next(label))
        yield
        parts = [piece, sequence.ready(got)]
        if extra and dims is hops[0]:
            parts.append(small)
        piece = jnp.concatenate(parts, axis=0)
    near = sequence.swap(piece, core, next(label))
    write(piece)
    yield
    write(piece, near)


def body(
    axes,
    tokens,
    norm1_gain,
    norm1_bias,
    qkv_weight,
    qv_bias,
    proj_weight,
    proj_bias,
    norm2_gain,
    norm2_bias,
    fc1_weight,
    fc1_bias,
    fc2_weight,
    fc2_bias,
    cotangent,
):
    items, steps, lat_dev, lon, width = tokens.shape
    hidden = fc1_weight.shape[1]
    rows = items * steps * lat_dev * lon
    side = items * steps * lon
    lat_total = axes.sizes["lat"]
    shards = 8
    odd = axes.bit(axes.core) == 1
    first = tokens[:, :, 0].reshape(side, width)
    last = tokens[:, :, lat_dev - 1].reshape(side, width)
    beside = axes.beside(jnp.where(odd, first, last))
    across = axes.across(jnp.where(odd, last, first))
    flat_tokens = tokens.reshape(rows, width)
    flat_cot = cotangent.reshape(rows, width)
    operands = (
        flat_tokens,
        norm1_gain,
        norm1_bias,
        qv_bias,
        beside,
        across,
        qkv_weight,
        proj_weight,
        proj_bias,
        norm2_gain,
        norm2_bias,
        fc1_weight,
        fc1_bias,
        fc2_weight,
        fc2_bias,
        flat_cot,
    )
    band = rows // items
    keys = band + 2 * side // items
    groups = width // 128
    both = hidden + width
    (mixed, a_low, dx1, small, keep1, send1, keep2, send2, dq, dk, dv, to_beside, to_across) = on_device(
        functools.partial(block_kernel, axes, shards, items, steps, lat_dev, lon),
        operands,
        [
            ((rows, width), bf16),
            ((rows, width), bf16),
            ((rows, width), f32),
            ((4 + hidden // width, width), f32),
            ((hidden // 2, width), bf16),
            ((hidden // 2, width), bf16),
            ((width // 2, both), bf16),
            ((width // 2, both), bf16),
            ((rows, width), bf16),
            ((rows, width), f32),
            ((rows, width), f32),
            ((2, side, width), bf16),
            ((2, side, width), bf16),
        ],
        scratch=[
            ((2, rows + 2 * side, width), bf16),
            ((rows, width), bf16),
            ((items * groups, GROUP * band, keys), f32),
            ((rows, width), bf16),
            ((rows, width), bf16),
            ((rows, width), bf16),
            ((rows, hidden), bf16),
            ((rows, hidden), bf16),
            ((rows, width), bf16),
        ],
        sems=[(16,), (13, items)],
        flops=2 * rows * width * (4 * width + 6 * hidden),
    )

    from_beside = axes.beside(to_beside)
    from_across = axes.across(to_across)
    sequence = Sequence(axes, (to_beside, to_across))
    grads = {}
    splits = {1: (width,), 2: (hidden, width), 3: (3 * width,)}

    last = {}
    rows_of = {1: hidden, 2: width, 3: width}

    def stream(name, keep, send, small=None):
        def write(own, other=None):
            if other is None:
                grads[name] = spread(axes, shards, ((name - 1, splits[name]),), (rows_of[name],), (own,))
                sequence.token = grads[name][0]
            last[name] = own, other

        return sum_stream(sequence, name - 1, keep, send, write, small)

    small_places = (
        (0, (width,)),
        (1, (width,)),
        (2, (2, width)),
        (7, (width,)),
        (4, (width,)),
        (5, (width,)),
        (8, (hidden,)),
        (6, (width,)),
    )
    streams = {1: stream(1, keep1, send1), 2: stream(2, keep2, send2)}
    next(streams[2])
    next(streams[1])
    sequence.token = from_beside

    def join():
        operands = (
            after(dq, sequence.token),
            dk,
            dv,
            from_beside,
            from_across,
            a_low,
            qkv_weight,
            flat_tokens,
            norm1_gain,
            dx1,
            small,
        )
        keep, send, grad, sums = on_device(
            functools.partial(qkv_grad_kernel, axes, shards, lat_dev, lon),
            operands,
            [
                ((width // 2, 3 * width), bf16),
                ((width // 2, 3 * width), bf16),
                ((rows, width), bf16),
                (((8 + hidden // width) // 3, 3 * width), bf16),
            ],
            scratch=[((rows, 3 * width), bf16)],
            sems=[(11,), (4,)],
            flops=12 * rows * width * width,
        )
        streams[3] = stream(3, keep, send, sums)
        return grad

    for name in ORDER + (1, 2, 3) * 12:
        if name not in streams:
            tokens_grad = join()
        next(streams[name], None)
    grad_fc2, grad_fc1, grad_proj, grad_qkv, *sums = spread(
        axes,
        shards,
        tuple((name - 1, splits[name]) for name in (1, 2, 3)),
        tuple(rows_of[name] for name in (1, 2, 3)),
        tuple(last[name][1] for name in (1, 2, 3)) + (last[3][0],),
        tuple(out for name in (1, 2, 3) for out in grads[name]),
        small_places,
    )
    return (
        mixed.reshape(tokens.shape),
        tokens_grad.reshape(tokens.shape),
        sums[0],
        sums[1],
        grad_qkv,
        sums[2],
        grad_proj,
        sums[3],
        sums[4],
        sums[5],
        grad_fc1,
        sums[6],
        grad_fc2,
        sums[7],
    )


def solution(mesh):
    split = P("items", None, "lat", None, None)
    whole = P()
    return jax.shard_map(
        functools.partial(body, Axes(mesh)),
        mesh=mesh,
        in_specs=(split,) + (whole,) * 12 + (split,),
        out_specs=(split, split) + (whole,) * 12,
        check_vma=False,
    )
```

```python
import functools
import math

import jax
import jax.numpy as jnp
from jax import lax
from jax.experimental import pallas as pl
from jax.experimental.pallas import tpu as pltpu
from jax.sharding import PartitionSpec as P

HEAD_DIM = 32
ROW_REACH = 1
COL_REACH = 2
GROUP = 128 // HEAD_DIM
EPSILON = 1e-06
SCALE = HEAD_DIM ** (-0.5)
SQRT_HALF = 0.5**0.5
PHI_SCALE = (2.0 * math.pi) ** (-0.5)
NEGATIVE = -1e30
CUT = 2048
PACE = 2
ORDERS = (("zxyw", "xyzw"), ("yzxw", "zywx"), ("yxzw", "xyzw"))
ORDER = (2, 3, 1, 3, 2, 1, 3, 2, 1, 3, 2, 1, 3, 2, 1, 2, 3, 1, 2, 3, 1, 3, 2, 1, 3, 2, 1, 3)

f32 = jnp.float32
bf16 = jnp.bfloat16
MIB = 1024 * 1024


def dot_nn(left, right):
    return lax.dot_general(left, right, (((1,), (0,)), ((), ())), preferred_element_type=f32)


def dot_nt(left, right):
    return lax.dot_general(left, right, (((1,), (1,)), ((), ())), preferred_element_type=f32)


def dot_tn(left, right):
    return lax.dot_general(left, right, (((0,), (0,)), ((), ())), preferred_element_type=f32)


def normed(values):
    mean = jnp.mean(values, axis=-1, keepdims=True)
    centred = values - mean
    spread = jnp.mean(centred * centred, axis=-1, keepdims=True)
    scale = lax.rsqrt(spread + EPSILON)
    return centred * scale, scale


def norm_back(grad, gain, unit, scale):
    scaled = grad * gain
    first = jnp.mean(scaled, axis=-1, keepdims=True)
    second = jnp.mean(scaled * unit, axis=-1, keepdims=True)
    return scale * (scaled - first - unit * second)


def as_row(ref):
    return ref[...].astype(f32).reshape(1, ref.shape[0])


def stack_heads(block, lane_head):
    zero = jnp.zeros_like(block)
    return jnp.concatenate(
        [jnp.where(lane_head == head, block, zero) for head in range(GROUP)], axis=0
    )


def fold_heads(stacked, lane_head, rows):
    total = jnp.where(lane_head == 0, stacked[:rows], 0.0)
    for head in range(1, GROUP):
        total = jnp.where(lane_head == head, stacked[head * rows : (head + 1) * rows], total)
    return total


def window_bias(axes, steps, lat_dev, lon):
    band = steps * lat_dev * lon
    keys = band + 2 * steps * lon
    query = lax.broadcasted_iota(jnp.int32, (band, keys), 0)
    key = lax.broadcasted_iota(jnp.int32, (band, keys), 1)
    query_row = query // lon % lat_dev
    first = jnp.where(axes.has_below(), -1, -2 - ROW_REACH)
    last = jnp.where(axes.has_above(), lat_dev, lat_dev + 1 + ROW_REACH)
    key_row = jnp.where(
        key < band, key // lon % lat_dev, jnp.where(key < band + steps * lon, first, last)
    )
    gap = jnp.abs(query % lon - key % lon)
    gap = jnp.minimum(gap, lon - gap)
    seen = (jnp.abs(query_row - key_row) <= ROW_REACH) & (gap <= COL_REACH)
    return jnp.where(seen, 0.0, NEGATIVE)


def block_kernel(
    axes,
    shards,
    items,
    steps,
    lat_dev,
    lon,
    *refs,
):
    sources, finals, refs = refs[:16], refs[16:29], refs[29:]
    targets, locals_, refs = refs[:16], refs[16:29], refs[29:]
    kv_ref, q_ref, p_ref, do_ref, o_ref, c_ref, g_ref, du_ref, dy_ref, in_sems, out_sems = refs
    fetches = start_copies(sources, targets, in_sems)
    (tok, gain1, bias1, qv_bias, beside, across, wqkv, wproj) = targets[:8]
    (bproj, gain2, bias2, w1, b1, w2, b2, cot) = targets[8:]
    (mixed_out, a_out, dx1_out, small_out, keep1, send1, keep2, send2) = locals_[:8]
    (dq_out, dk_out, dv_out, to_beside, to_across) = locals_[8:]
    leaving = []

    def leave(index, slot=0, window=None):
        source, target = locals_[index], finals[index]
        if window is not None:
            source, target = source.at[window], target.at[window]
        copy = pltpu.make_async_copy(source, target, out_sems.at[index, slot])
        copy.start()
        leaving.append(copy)

    for copy in fetches[:6]:
        copy.wait()
    rows, width = tok.shape
    hidden = w1.shape[1]
    side = beside.shape[0]
    band = rows // items
    edge = side // items
    groups = width // 128
    lane_head = lax.broadcasted_iota(jnp.int32, (1, 128), 1) // HEAD_DIM

    g1 = as_row(gain1)
    h1 = as_row(bias1)
    x = tok[...].astype(f32)
    unit, _ = normed(x)
    a_own = (unit * g1 + h1).astype(bf16)
    a_out[...] = a_own
    leave(1)
    wide = jnp.concatenate([beside[...], across[...]], axis=0).astype(f32)
    unit_wide, _ = normed(wide)
    a_wide = (unit_wide * g1 + h1).astype(bf16)
    a_all = jnp.concatenate([a_own, a_wide], axis=0)
    fetches[6].wait()
    q_ref[...] = (dot_nn(a_own, wqkv[:, :width]) + qv_bias[0:1, :].astype(f32)).astype(bf16)
    kv_ref[0] = dot_nn(a_all, wqkv[:, width : 2 * width]).astype(bf16)
    kv_ref[1] = (dot_nn(a_all, wqkv[:, 2 * width :]) + qv_bias[1:2, :].astype(f32)).astype(bf16)

    window = jnp.concatenate([window_bias(axes, steps, lat_dev, lon)] * GROUP, axis=0)
    odd = axes.bit(axes.core)
    below = pl.multiple_of(rows + (1 - odd) * side, 16)
    above = pl.multiple_of(rows + odd * side, 16)

    def keys_of(which, item, lanes):
        return jnp.concatenate(
            [
                kv_ref[which, item * band : (item + 1) * band, lanes],
                kv_ref[which, pl.ds(below + item * edge, edge), lanes],
                kv_ref[which, pl.ds(above + item * edge, edge), lanes],
            ],
            axis=0,
        )

    for item in range(items):
        for group in range(groups):
            lanes = slice(group * 128, (group + 1) * 128)
            own = slice(item * band, (item + 1) * band)
            queries = stack_heads(q_ref[own, lanes], lane_head)
            scores = dot_nt(queries, keys_of(0, item, lanes)) * SCALE + window
            top = jnp.max(scores, axis=-1, keepdims=True)
            weights = jnp.exp(scores - top)
            total = jnp.sum(weights, axis=-1, keepdims=True)
            soft = weights * (1.0 / total)
            p_ref[item * groups + group] = soft
            mixed_heads = dot_nn(soft.astype(bf16), keys_of(1, item, lanes))
            o_ref[own, lanes] = fold_heads(mixed_heads, lane_head, band).astype(bf16)

    for copy in fetches[7:]:
        copy.wait()
    g2 = as_row(gain2)
    h2 = as_row(bias2)
    x1 = x + dot_nn(o_ref[...], wproj[...]) + as_row(bproj)
    unit2, scale2 = normed(x1)
    c_low = (unit2 * g2 + h2).astype(bf16)
    c_ref[...] = c_low
    cot_low = cot[...]
    branch = jnp.zeros((rows, width), f32)
    dc = jnp.zeros((rows, width), f32)
    b1_row = as_row(b1)
    for start in range(0, hidden, 2048):
        cols = slice(start, start + 2048)
        u = dot_nn(c_low, w1[:, cols]) + b1_row[:, cols]
        cdf = 0.5 + 0.5 * lax.erf(u * SQRT_HALF)
        slope = cdf + u * (jnp.exp(u * u * -0.5) * PHI_SCALE)
        act = (u * cdf).astype(bf16)
        g_ref[:, cols] = act
        branch = branch + dot_nn(act, w2[cols, :])
        dh = dot_nt(cot_low, w2[cols, :])
        du_low = (dh * slope).astype(bf16)
        du_ref[:, cols] = du_low
        sums = jnp.sum(du_low.astype(f32), axis=0, keepdims=True)
        for row in range(sums.shape[1] // width):
            place = 4 + start // width + row
            small_out[place : place + 1, :] = sums[:, row * width : (row + 1) * width]
        dc = dc + dot_nt(du_low, w1[:, cols])
    mixed_out[...] = (x1 + branch + as_row(b2)).astype(bf16)
    cot_wide = cot_low.astype(f32)
    small_out[0:1, :] = jnp.sum(dc * unit2, axis=0, keepdims=True)
    small_out[1:2, :] = jnp.sum(dc, axis=0, keepdims=True)
    small_out[2:3, :] = jnp.sum(cot_wide, axis=0, keepdims=True)
    dx1 = cot_wide + norm_back(dc, g2, unit2, scale2)
    dx1_out[...] = dx1
    leave(0)
    leave(2)
    dy = dx1.astype(bf16)
    dy_ref[...] = dy
    small_out[3:4, :] = jnp.sum(dy.astype(f32), axis=0, keepdims=True)
    do_ref[...] = dot_nt(dy, wproj[...]).astype(bf16)
    leave(3)
    jobs = grad_jobs(axes, 1, shards, c_ref, du_ref, keep2, send2)
    jobs += grad_jobs(axes, 1, shards, o_ref, dy_ref, keep2, send2, hidden)
    jobs.append(lambda: (leave(6), leave(7)))
    jobs += grad_jobs(axes, 0, shards, g_ref, cot, keep1, send1)
    jobs.append(lambda: (leave(4), leave(5)))

    for item in range(items):
        for group in range(groups):
            lanes = slice(group * 128, (group + 1) * 128)
            own = slice(item * band, (item + 1) * band)
            ends = slice(item * edge, (item + 1) * edge)
            for _ in range(PACE):
                if jobs:
                    jobs.pop(0)()
            grads = stack_heads(do_ref[own, lanes], lane_head)
            queries = stack_heads(q_ref[own, lanes], lane_head)
            soft = p_ref[item * groups + group]
            dp = dot_nt(grads, keys_of(1, item, lanes))
            inner = jnp.sum(soft * dp, axis=-1, keepdims=True)
            ds = (soft * (dp - inner)).astype(bf16)
            dq = fold_heads(dot_nn(ds, keys_of(0, item, lanes)), lane_head, band) * SCALE
            dq_out[own, lanes] = dq.astype(bf16)
            dk = dot_tn(ds, queries) * SCALE
            dv = dot_tn(soft.astype(bf16), grads)
            dk_out[own, lanes] = dk[:band]
            dv_out[own, lanes] = dv[:band]
            for index, grad in ((0, dk), (1, dv)):
                down = grad[band : band + edge]
                up = grad[band + edge :]
                to_beside[index, ends, lanes] = jnp.where(odd == 1, down, up).astype(bf16)
                to_across[index, ends, lanes] = jnp.where(odd == 1, up, down).astype(bf16)
        for index in (8, 9, 10):
            leave(index, item, (own, slice(None)))
        for index in (11, 12):
            leave(index, item, (slice(None), ends, slice(None)))
    for copy in leaving:
        copy.wait()


def start_copies(sources, targets, sems, first=0):
    copies = [
        pltpu.make_async_copy(source, target, sems.at[first + index])
        for index, (source, target) in enumerate(zip(sources, targets))
    ]
    for copy in copies:
        copy.start()
    return copies


def grad_jobs(axes, stream, shards, left, right, keep, send, first=0):
    half = left.shape[1] // 2
    per = half // shards
    step = min(half, 256)
    width = min(right.shape[1], CUT)
    core = axes.bit(axes.core)
    jobs = []
    for ref, owner in ((keep, core), (send, 1 - core)):
        slot = axes.slot(stream, owner)
        for start in range(0, half, step):
            for column in range(0, right.shape[1], width):

                def job(ref=ref, owner=owner, slot=slot, start=start, column=column):
                    columns = pl.ds(pl.multiple_of(owner * half + start, 128), step)
                    end = min(column + width, right.shape[1])
                    product = dot_tn(left[:, columns], right[:, column:end])
                    lanes = slice(first + column, first + end)
                    for index in range(step // per):
                        spot = pl.multiple_of(((start // per + index) ^ slot) * per, per)
                        rows = slice(index * per, (index + 1) * per)
                        ref[pl.ds(spot, per), lanes] = product[rows].astype(bf16)

                jobs.append(job)
    return jobs


def qkv_grad_kernel(
    axes,
    shards,
    lat_dev,
    lon,
    *refs,
):
    sources, finals, refs = refs[:11], refs[11:15], refs[15:]
    targets, locals_, refs = refs[:11], refs[11:15], refs[15:]
    joined, in_sems, out_sems = refs
    fetches = start_copies(sources, targets, in_sems)
    dq, dk, dv, from_beside, from_across, a_low, wqkv, tok, gain1, dx1, small_in = targets
    keep, send, tokens_out, small_out = locals_
    for copy in fetches[:6]:
        copy.wait()
    rows, width = tok.shape
    joined[:, :width] = dq[...]
    odd = axes.bit(axes.core) == 1
    for which, grads in ((0, dk), (1, dv)):
        columns = slice((1 + which) * width, (2 + which) * width)
        for strip in range(rows // (lat_dev * lon)):
            edge = slice(strip * lon, (strip + 1) * lon)
            for row in range(lat_dev):
                start = (strip * lat_dev + row) * lon
                value = grads[start : start + lon, :]
                near = from_beside[which, edge, :].astype(f32)
                far = from_across[which, edge, :].astype(f32)
                if row == 0:
                    value = value + jnp.where(odd, near, far)
                if row == lat_dev - 1:
                    value = value + jnp.where(odd, far, near)
                joined[start : start + lon, columns] = value.astype(bf16)
    for job in grad_jobs(axes, 2, shards, a_low, joined, keep, send):
        job()
    leaving = start_copies(locals_[:2], finals[:2], out_sems)
    for copy in fetches[6:]:
        copy.wait()
    da = dot_nt(joined[...], wqkv[...])
    unit, scale = normed(tok[...].astype(f32))
    grad = dx1[...] + norm_back(da, as_row(gain1), unit, scale)
    tokens_out[...] = grad.astype(bf16)
    sums = [
        jnp.sum(da * unit, axis=0, keepdims=True),
        jnp.sum(da, axis=0, keepdims=True),
        jnp.sum(joined[:, :width].astype(f32), axis=0, keepdims=True),
        jnp.sum(joined[:, 2 * width :].astype(f32), axis=0, keepdims=True),
    ] + [small_in[index : index + 1, :] for index in range(small_in.shape[0])]
    for index, row in enumerate(sums):
        place_of = slice(index % 3 * width, (index % 3 + 1) * width)
        small_out[index // 3 : index // 3 + 1, place_of] = row.astype(bf16)
    leaving += start_copies(locals_[2:], finals[2:], out_sems, 2)
    for copy in leaving:
        copy.wait()


def spread_kernel(axes, shards, streams, other, sums, *refs):
    count = sum(len(widths) for _, widths in streams)
    pieces = refs[: len(streams)]
    outs = refs[-2 * (count + len(sums)) - 1 : -count - len(sums) - 1]
    wide, sems = refs[-count - len(sums) - 1 : -1], refs[-1]
    core = axes.bit(axes.core)
    owner = 1 - core if other else core
    copies = []

    def leave(source, target, index, part):
        copy = pltpu.make_async_copy(source, target, sems.at[index, part])
        copy.start()
        copies.append(copy)

    number = 0
    for piece, (stream, widths) in zip(pieces, streams):
        slot = axes.slot(stream, owner)
        per = outs[number].shape[0] // (2 * shards)
        for index in range(shards):
            spot = pl.multiple_of((owner * shards + (index ^ slot)) * per, per)
            rows = slice(index * per, (index + 1) * per)
            first = 0
            for part, width in enumerate(widths, number):
                wide[part][rows, :] = piece[rows, first : first + width].astype(f32)
                first += width
                leave(wide[part].at[rows, :], outs[part].at[pl.ds(spot, per), :], index, part)
        number += len(widths)
    if sums:
        rows = slice(shards * per, pieces[-1].shape[0])
        total = refs[len(streams)][rows, :].astype(f32) + pieces[-1][rows, :].astype(f32)
        width = total.shape[1] // 3
        taken = [
            total[k // 3 : k // 3 + 1, k % 3 * width : (k % 3 + 1) * width]
            for k in range(3 * total.shape[0])
        ]
        for part, (first, shape) in enumerate(sums):
            buffer = wide[count + part]
            for k in range(math.prod(shape) // width):
                if len(shape) == 1:
                    buffer[k * width : (k + 1) * width] = taken[first + k].reshape(width)
                else:
                    buffer[k : k + 1, :] = taken[first + k]
            leave(buffer, outs[count + part], part, count)
    for copy in copies:
        copy.wait()


def spread(axes, shards, streams, rows, pieces, outs=(), sums=()):
    hbm = pl.BlockSpec(memory_space=pltpu.HBM)
    shapes = [(count, width) for (_, widths), count in zip(streams, rows) for width in widths]
    halves = [(count // 2, width) for count, width in shapes]
    shapes += [shape for _, shape in sums]
    return pl.pallas_call(
        functools.partial(spread_kernel, axes, shards, streams, bool(outs), sums),
        out_shape=[jax.ShapeDtypeStruct(shape, f32) for shape in shapes],
        in_specs=[pl.BlockSpec(memory_space=pltpu.VMEM)] * len(pieces) + [hbm] * len(outs),
        out_specs=[hbm] * len(shapes),
        scratch_shapes=[pltpu.VMEM(shape, f32) for shape in halves]
        + [pltpu.VMEM(shape, f32) for _, shape in sums]
        + [pltpu.SemaphoreType.DMA((max(shards, len(sums)), len(halves) + 1))],
        input_output_aliases={len(pieces) + index: index for index in range(len(outs))},
        compiler_params=pltpu.CompilerParams(vmem_limit_bytes=(4 + 4 * len(streams)) * MIB),
        cost_estimate=pl.CostEstimate(
            flops=0,
            bytes_accessed=6 * sum(math.prod(shape) for shape in halves),
            transcendentals=0,
        ),
    )(*pieces, *outs)


def on_device(kernel, operands, outs, scratch=(), sems=(), flops=0):
    buffers = [pltpu.VMEM(value.shape, value.dtype) for value in operands]
    buffers += [pltpu.VMEM(shape, jnp.dtype(dtype)) for shape, dtype in outs]
    hbm = pl.BlockSpec(memory_space=pltpu.HBM)
    return pl.pallas_call(
        kernel,
        out_shape=[jax.ShapeDtypeStruct(shape, dtype) for shape, dtype in outs],
        in_specs=[hbm] * len(operands),
        out_specs=[hbm] * len(outs),
        scratch_shapes=buffers
        + [pltpu.VMEM(shape, dtype) for shape, dtype in scratch]
        + [pltpu.SemaphoreType.DMA(shape) for shape in sems],
        compiler_params=pltpu.CompilerParams(vmem_limit_bytes=60 * MIB),
        cost_estimate=pl.CostEstimate(
            flops=flops,
            bytes_accessed=sum(math.prod(buffer.shape) * buffer.dtype.itemsize for buffer in buffers),
            transcendentals=0,
        ),
    )(*operands)


class Axes:
    def __init__(self, mesh):
        self.sizes = dict(mesh.shape)
        bits = self.sizes["items"].bit_length() - 1
        self.core = ("lat", 1)
        named = {"x": ("lat", 2), "y": ("items", 1), "z": ("items", 2), "w": ("items", 4)}
        self.orders = [[[named[key] for key in order] for order in pair] for pair in ORDERS]
        self.extra = [("items", 1 << bit) for bit in range(3, bits)]

    def bit(self, dim):
        axis, value = dim
        return (lax.axis_index(axis) // value) % 2

    def slot(self, stream, core):
        pair = []
        for order in self.orders[stream]:
            total = 0
            for dim in order[:-1]:
                total = total * 2 + self.bit(dim)
            pair.append(total)
        return jnp.where(core == 0, pair[0], pair[1])

    def has_below(self):
        return lax.axis_index("lat") > 0

    def has_above(self):
        return lax.axis_index("lat") < self.sizes["lat"] - 1

    def beside(self, value):
        return self.exchange(value, (self.core, self.core))

    def across(self, value):
        count = self.sizes["lat"]
        pairs = [(index, (index + 1) // 2 * 4 - 1 - index) for index in range(1, count - 1)]
        return lax.ppermute(value, "lat", pairs)

    def exchange(self, value, dims):
        items = self.sizes["items"]
        pairs = []
        for index in range(self.sizes["lat"] * items):
            axis, bit = dims[index // items % 2]
            pairs.append((index, index ^ (bit * items if axis == "lat" else bit)))
        return lax.ppermute(value, ("lat", "items"), pairs)


def add_rows(terms, low, high):
    total = terms[0][low:high].astype(f32)
    for term in terms[1:]:
        total = total + term[low:high].astype(f32)
    return total


def after(value, token):
    return lax.optimization_barrier((value, token))[0]


class Sequence:
    def __init__(self, axes, token):
        self.axes = axes
        self.token = token

    def ready(self, value):
        return after(value, self.token)

    def swap(self, value, dims, scope="swap"):
        self.token = value
        with jax.named_scope(scope):
            return self.axes.exchange(value, dims)


def sum_stream(sequence, stream, keep, send, write, small=None):
    axes = sequence.axes
    core = (axes.core, axes.core)
    label = (f"s{stream + 1}h{hop}" for hop in range(99))
    got = sequence.swap(send, core, next(label))
    yield
    terms = [keep, sequence.ready(got)]
    rows = keep.shape[0]
    extra = 0 if small is None else small.shape[0]
    pairs = list(zip(*axes.orders[stream]))
    hops, whole = pairs[:-1], pairs[-1:] + [(dim, dim) for dim in axes.extra]
    for dims in hops:
        rows //= 2
        value = add_rows(terms, rows, 2 * rows).astype(bf16)
        if extra:
            value = jnp.concatenate([value, small], axis=0)
        got = sequence.swap(value, dims, next(label))
        yield
        got = sequence.ready(got)
        if extra:
            small = (small.astype(f32) + got[rows:].astype(f32)).astype(bf16)
        terms.append(got)
    piece = add_rows(terms, 0, rows).astype(bf16)
    for dims in whole:
        value = jnp.concatenate([piece, small], axis=0) if extra else piece
        got = sequence.swap(value, dims, next(label))
        yield
        got = sequence.ready(got)
        if extra:
            small = (small.astype(f32) + got[rows:].astype(f32)).astype(bf16)
        piece = (piece.astype(f32) + got[:rows].astype(f32)).astype(bf16)
    for dims in reversed(hops):
        got = sequence.swap(piece, dims, next(label))
        yield
        parts = [piece, sequence.ready(got)]
        if extra and dims is hops[0]:
            parts.append(small)
        piece = jnp.concatenate(parts, axis=0)
    near = sequence.swap(piece, core, next(label))
    write(piece)
    yield
    write(piece, near)


def body(
    axes,
    tokens,
    norm1_gain,
    norm1_bias,
    qkv_weight,
    qv_bias,
    proj_weight,
    proj_bias,
    norm2_gain,
    norm2_bias,
    fc1_weight,
    fc1_bias,
    fc2_weight,
    fc2_bias,
    cotangent,
):
    items, steps, lat_dev, lon, width = tokens.shape
    hidden = fc1_weight.shape[1]
    rows = items * steps * lat_dev * lon
    side = items * steps * lon
    lat_total = axes.sizes["lat"]
    shards = 8
    odd = axes.bit(axes.core) == 1
    first = tokens[:, :, 0].reshape(side, width)
    last = tokens[:, :, lat_dev - 1].reshape(side, width)
    beside = axes.beside(jnp.where(odd, first, last))
    across = axes.across(jnp.where(odd, last, first))
    flat_tokens = tokens.reshape(rows, width)
    flat_cot = cotangent.reshape(rows, width)
    operands = (
        flat_tokens,
        norm1_gain,
        norm1_bias,
        qv_bias,
        beside,
        across,
        qkv_weight,
        proj_weight,
        proj_bias,
        norm2_gain,
        norm2_bias,
        fc1_weight,
        fc1_bias,
        fc2_weight,
        fc2_bias,
        flat_cot,
    )
    band = rows // items
    keys = band + 2 * side // items
    groups = width // 128
    both = hidden + width
    (mixed, a_low, dx1, small, keep1, send1, keep2, send2, dq, dk, dv, to_beside, to_across) = on_device(
        functools.partial(block_kernel, axes, shards, items, steps, lat_dev, lon),
        operands,
        [
            ((rows, width), bf16),
            ((rows, width), bf16),
            ((rows, width), f32),
            ((4 + hidden // width, width), f32),
            ((hidden // 2, width), bf16),
            ((hidden // 2, width), bf16),
            ((width // 2, both), bf16),
            ((width // 2, both), bf16),
            ((rows, width), bf16),
            ((rows, width), f32),
            ((rows, width), f32),
            ((2, side, width), bf16),
            ((2, side, width), bf16),
        ],
        scratch=[
            ((2, rows + 2 * side, width), bf16),
            ((rows, width), bf16),
            ((items * groups, GROUP * band, keys), f32),
            ((rows, width), bf16),
            ((rows, width), bf16),
            ((rows, width), bf16),
            ((rows, hidden), bf16),
            ((rows, hidden), bf16),
            ((rows, width), bf16),
        ],
        sems=[(16,), (13, items)],
        flops=2 * rows * width * (4 * width + 6 * hidden),
    )

    from_beside = axes.beside(to_beside)
    from_across = axes.across(to_across)
    sequence = Sequence(axes, (to_beside, to_across))
    grads = {}
    splits = {1: (width,), 2: (hidden, width), 3: (3 * width,)}

    last = {}
    rows_of = {1: hidden, 2: width, 3: width}

    def stream(name, keep, send, small=None):
        def write(own, other=None):
            if other is None:
                grads[name] = spread(axes, shards, ((name - 1, splits[name]),), (rows_of[name],), (own,))
                sequence.token = grads[name][0]
            last[name] = own, other

        return sum_stream(sequence, name - 1, keep, send, write, small)

    small_places = (
        (0, (width,)),
        (1, (width,)),
        (2, (2, width)),
        (7, (width,)),
        (4, (width,)),
        (5, (width,)),
        (8, (hidden,)),
        (6, (width,)),
    )
    streams = {1: stream(1, keep1, send1), 2: stream(2, keep2, send2)}
    next(streams[2])
    next(streams[1])
    sequence.token = from_beside

    def join():
        operands = (
            after(dq, sequence.token),
            dk,
            dv,
            from_beside,
            from_across,
            a_low,
            qkv_weight,
            flat_tokens,
            norm1_gain,
            dx1,
            small,
        )
        keep, send, grad, sums = on_device(
            functools.partial(qkv_grad_kernel, axes, shards, lat_dev, lon),
            operands,
            [
                ((width // 2, 3 * width), bf16),
                ((width // 2, 3 * width), bf16),
                ((rows, width), bf16),
                (((8 + hidden // width) // 3, 3 * width), bf16),
            ],
            scratch=[((rows, 3 * width), bf16)],
            sems=[(11,), (4,)],
            flops=12 * rows * width * width,
        )
        streams[3] = stream(3, keep, send, sums)
        return grad

    for name in ORDER + (1, 2, 3) * 12:
        if name not in streams:
            tokens_grad = join()
        next(streams[name], None)
    grad_fc2, grad_fc1, grad_proj, grad_qkv, *sums = spread(
        axes,
        shards,
        tuple((name - 1, splits[name]) for name in (1, 2, 3)),
        tuple(rows_of[name] for name in (1, 2, 3)),
        tuple(last[name][1] for name in (1, 2, 3)) + (last[3][0],),
        tuple(out for name in (1, 2, 3) for out in grads[name]),
        small_places,
    )
    return (
        mixed.reshape(tokens.shape),
        tokens_grad.reshape(tokens.shape),
        sums[0],
        sums[1],
        grad_qkv,
        sums[2],
        grad_proj,
        sums[3],
        sums[4],
        sums[5],
        grad_fc1,
        sums[6],
        grad_fc2,
        sums[7],
    )


def solution(mesh):
    split = P("items", None, "lat", None, None)
    whole = P()
    return jax.shard_map(
        functools.partial(body, Axes(mesh)),
        mesh=mesh,
        in_specs=(split,) + (whole,) * 12 + (split,),
        out_specs=(split, split) + (whole,) * 12,
        check_vma=False,
    )
```
